1024 devices in a mesh: dp: 8 (over x, y_hi), tensor: 128 (over z, y_lo, core).
Axes of the slice: x: 4, y: 4 (y_hi: 2, y_lo: 2; y = y_hi * 2 + y_lo), z: 32, core: 2. Of those that a mesh axis runs over, the one named last changes fastest.
Arguments:
- context: bfloat16 [1024, 6144], P('dp', 'tensor'), may hold values from -6 to 6
- w_out: bfloat16 [18432, 6144], P('tensor'), may hold values from -0.3125 to 0.3125
- out_grad: bfloat16 [1024, 18432], P('dp', 'tensor'), may hold values from -6 to 6
Outputs:
- projected: bfloat16 [1024, 18432], P('dp', 'tensor')
- context_grad: bfloat16 [1024, 6144], P('dp', 'tensor')
- weight_grad: float32 [18432, 6144], P('tensor', 'dp')
The draws below stay inside these ranges and needn't reach their ends.
All inputs are finite; a program needn't handle non-finite values.
Results may differ from the reference program's by a relative error of at most 0.0085.
Values may be sent and summed in bfloat16 or wider, within the bound.
A program may use at most 32 MiB of HBM per device.

```python
import jax
import jax.numpy as jnp
from jax import lax

D = 18432
TOK = 128
QW = 6144
TOKENS = 1024


def strengthened(result, own_key, source, target, shards_of, factor):
    def block_of(axis_at):
        return (jnp.arange(result.shape[axis_at]) // (result.shape[axis_at] // shards_of)).reshape((-1,) + (1,) * (result.ndim - 1 - axis_at))

    near = jax.random.permutation(own_key, shards_of)[block_of(target)]
    second = (block_of(target) + shards_of // 2) % shards_of
    return jnp.where((block_of(source) == near) | (block_of(source) == second), factor * result, result)


def level_of(own_key, extent, shards, least, top_value):
    def one(dim, parts):
        draws = jax.random.uniform(jax.random.fold_in(jax.random.fold_in(own_key, 6), dim), (parts,), jnp.float32, least / len(shards), top_value / len(shards))
        return jnp.repeat(jnp.exp(draws), extent[dim] // parts).reshape((-1,) + (1,) * (len(extent) - dim - 1))

    gain = one(*shards[0])
    for cut in shards[1:]:
        gain = gain * one(*cut)
    return gain


def gaussian(stream_key, shape, deviation, limit, split=(), dtype=jnp.bfloat16):
    drawn = deviation * jax.random.normal(stream_key, shape, jnp.float32)
    if split:
        drawn = drawn * level_of(stream_key, shape, split, -0.22, 0.18)
    return jnp.clip(drawn, -limit, limit).astype(dtype)


def bell_draw_with(key, extent, deviation, most, split, heavy, held_as=jnp.bfloat16):
    entries = deviation * jax.random.normal(key, extent, jnp.float32)
    if split:
        entries = entries * level_of(key, extent, split, -0.22, 0.18)
    return jnp.clip(strengthened(entries, jax.random.fold_in(key, 3), *heavy), -most, most).astype(held_as)


def setup_inputs(seed: int = 0) -> dict:
    seeds = jax.random.split(jax.random.key(seed), 4)
    return {
        "context": gaussian(seeds[0], (TOKENS, QW), 1.0, 6.0, ((0, 8), (1, 128))),
        "w_out": bell_draw_with(seeds[1], (D, QW), QW ** -0.5, 0.3125, ((0, 128),), (0, 1, 128, 5.5)),
        "out_grad": gaussian(seeds[2], (TOKENS, D), 1.0, 6.0, ((0, 8), (1, 128))),
    }


def reference(context, w_out, out_grad):
    projected = lax.dot_general(context, w_out, (((1,), (1,)), ((), ())), preferred_element_type=jnp.float32).astype(jnp.bfloat16)
    context_grad = jnp.dot(out_grad, w_out, preferred_element_type=jnp.float32).astype(jnp.bfloat16)
    replicas = context.shape[0] // TOK
    context_sets = context.reshape(replicas, TOK, QW)
    grad_sets = out_grad.reshape(replicas, TOK, D)

    def accumulate(running, pair):
        seg_context, seg_grad = pair
        partial_value = lax.dot_general(seg_grad, seg_context, (((0,), (0,)), ((), ())), preferred_element_type=jnp.float32).astype(jnp.bfloat16)
        partial_value = lax.optimization_barrier(partial_value)
        return running + partial_value.astype(jnp.float32), None

    weight_grad, _ = lax.scan(accumulate, jnp.zeros((D, QW), jnp.float32), (context_sets, grad_sets))
    return projected, context_grad, weight_grad
```

```python
import jax
import jax.numpy as jnp
from jax import lax
from jax.experimental import pallas as pl
from jax.experimental.pallas import tpu as pltpu
from jax.sharding import PartitionSpec as P

MESH = pl.DeviceIdType.MESH
F32, BF16 = jnp.float32, jnp.bfloat16
R, G, Q, S, FB, TOK, ROWS = 8, 8, 4, 4, 48, 128, 144


def dot_nt(a, b):
    return lax.dot_general(a, b, (((1,), (1,)), ((), ())), preferred_element_type=F32)


def eye(n):
    return (
        lax.broadcasted_iota(jnp.int32, (n, n), 0) == lax.broadcasted_iota(jnp.int32, (n, n), 1)
    ).astype(F32).astype(BF16)


def kernel(
    ctx, w, og, proj, cg, wg,
    xt, pf, pc, rc, ysend, yrecv, nsend, nrecv, fsend, frecv, oga, x2,
    fa_s, fa_r, na_s, na_r, ya_s, ya_r, ca_s, ca_r, cb_s, cb_r, og_s, og_r, x_s, x_r, xc_s, xc_r,
    rc_s, rc_r, ry_s, ry_r, rn_s, rn_r, rf_s, rf_r,
):
    r = lax.axis_index("dp")
    t = lax.axis_index("tensor")
    z, s = t // 4, t % 4
    yl, c = s // 2, s % 2
    q, g = z % 4, z // 4
    sib = 2 * yl + (1 - c)
    par = 2 * (1 - yl) + c

    def at_z(d):
        return (r, ((z + d + 32) % 32) * 4 + s)

    core_dev, y_dev = (r, z * 4 + sib), (r, z * 4 + par)

    def rep(k, sp):
        return ((r + k) % R, z * 4 + sp)

    barrier = pltpu.get_barrier_semaphore()
    partners = [at_z(4 * k) for k in range(1, G)] + [at_z(d) for d in (1, -1, 2, -2)] + [core_dev, y_dev]
    partners += [rep(k, sp) for k in range(1, R) for sp in (s, par)]
    for device in partners:
        pl.semaphore_signal(barrier, inc=1, device_id=device, device_id_type=MESH)

    xt[g, q, s] = dot_nt(eye(FB), ctx[...]).astype(BF16)
    oga[r] = dot_nt(eye(ROWS), og[...]).astype(BF16)

    for j in range(16):
        part = jnp.dot(og[...], w[:, j * 384 : (j + 1) * 384], preferred_element_type=F32)
        part = part.T.reshape(2, S, FB, TOK)
        for i in range(2):
            zz = 2 * j + i
            pf[zz % 4, zz // 4] = part[i]
    for cls in range(Q):
        for y in range(2):
            pc[cls, y] = pf[cls, :, 2 * y + 1 - c].astype(BF16)

    pl.semaphore_wait(barrier, len(partners))

    pending = []

    def send(src, dst, ssem, rsem, device):
        copy = pltpu.make_async_remote_copy(
            src_ref=src, dst_ref=dst, send_sem=ssem, recv_sem=rsem, device_id=device, device_id_type=MESH
        )
        copy.start()
        pending.append(copy)

    def arrived(dst, ssem, rsem):
        pltpu.make_async_remote_copy(
            src_ref=dst, dst_ref=dst, send_sem=ssem, recv_sem=rsem, device_id=core_dev, device_id_type=MESH
        ).wait_recv()

    for k in (4, 3, 5, 2, 6, 1, 7):
        block = xt.at[g, q, s]
        send(block, block, fa_s.at[k], fa_r.at[g], at_z(4 * k))
    order = [(q + 2) % 4, (q + 1) % 4, (q + 3) % 4, q]
    for i, cls in enumerate(order):
        send(pc.at[cls], rc.at[cls], rc_s.at[i], rc_r.at[i], core_dev)
    for k in range(1, R):
        send(oga.at[r], oga.at[r], og_s.at[k], og_r.at[r], rep(k, s))

    for i, cls in enumerate(order):
        arrived(rc.at[cls], rc_s.at[i], rc_r.at[i])
        ysend[cls] = (pf[cls, :, par] + rc[cls, 1 - yl].astype(F32)).astype(BF16)
        send(ysend.at[cls], yrecv.at[cls], ry_s.at[i], ry_r.at[i], y_dev)
    for i, cls in enumerate(order):
        arrived(yrecv.at[cls], ry_s.at[i], ry_r.at[i])
        total = pf[cls, :, s] + rc[cls, yl].astype(F32) + yrecv[cls].astype(F32)
        if i == 3:
            pf[cls, :, s] = total
        else:
            nsend[i] = total.astype(BF16)
            if i == 0:
                send(nsend.at[0, 0:4], nrecv.at[0, 0:4], rn_s.at[0], rn_r.at[0], at_z(2))
                send(nsend.at[0, 4:8], nrecv.at[0, 4:8], rn_s.at[1], rn_r.at[1], at_z(-2))
            else:
                send(nsend.at[i], nrecv.at[i], rn_s.at[i + 1], rn_r.at[i + 1], at_z(1 if i == 1 else -1))

    for k in range(1, G):
        gg = (g + k) % G
        arrived(xt.at[gg, q, s], fa_s.at[k], fa_r.at[gg])
    own, half0, half1 = xt.at[:, q, s], xt.at[0:4, q, s], xt.at[4:8, q, s]
    send(own, own, na_s.at[0], na_r.at[0], at_z(1))
    send(own, own, na_s.at[1], na_r.at[1], at_z(-1))
    send(half0, half0, na_s.at[2], na_r.at[2], at_z(2))
    send(half1, half1, na_s.at[3], na_r.at[3], at_z(-2))

    def spread(i, cls):
        mine = xt.at[:, cls, s]
        send(mine, mine, ya_s.at[i], ya_r.at[i], y_dev)
        send(mine, mine, ca_s.at[i], ca_r.at[i], core_dev)

    spread(0, q)

    arrived(nrecv.at[0, 0:4], rn_s.at[0], rn_r.at[0])
    arrived(nrecv.at[0, 4:8], rn_s.at[1], rn_r.at[1])
    arrived(nrecv.at[1], rn_s.at[2], rn_r.at[2])
    arrived(nrecv.at[2], rn_s.at[3], rn_r.at[3])
    window = pf[q, :, s] + nrecv[0].astype(F32) + nrecv[1].astype(F32) + nrecv[2].astype(F32)
    pf[q, :, s] = window
    fsend[...] = window.astype(BF16)
    for k in (4, 3, 5, 2, 6, 1, 7):
        gg = (g + k) % G
        send(fsend.at[gg], frecv.at[g], rf_s.at[k], rf_r.at[g], at_z(4 * k))

    arrived(xt.at[:, (q + 3) % 4, s], na_s.at[0], na_r.at[0])
    arrived(xt.at[:, (q + 1) % 4, s], na_s.at[1], na_r.at[1])
    arrived(xt.at[0:4, (q + 2) % 4, s], na_s.at[2], na_r.at[2])
    arrived(xt.at[4:8, (q + 2) % 4, s], na_s.at[3], na_r.at[3])
    for k in range(1, R):
        rr = (r + k) % R
        for j, sp in enumerate((s, par)):
            send(xt.at[rr, :, s], x2.at[r, :, s], x_s.at[k, j], x_r.at[r, yl], rep(k, sp))
    classes = [q, (q + 3) % 4, (q + 1) % 4, (q + 2) % 4]
    for i in range(1, Q):
        spread(i, classes[i])

    for k in range(1, R):
        gg = (r + k) % R
        arrived(oga.at[gg], og_s.at[k], og_r.at[gg])
    for i, cls in enumerate(classes):
        theirs = xt.at[:, cls, par]
        arrived(theirs, ya_s.at[i], ya_r.at[i])
        send(theirs, theirs, cb_s.at[i], cb_r.at[i], core_dev)

    for k in range(1, R):
        rr = (r + k) % R
        for y in range(2):
            piece = x2.at[rr, :, 2 * y + c]
            arrived(piece, x_s.at[k, y], x_r.at[rr, y])
            send(piece, piece, xc_s.at[k, y], xc_r.at[k, y], core_dev)

    for i, cls in enumerate(classes):
        arrived(xt.at[:, cls, sib], ca_s.at[i], ca_r.at[i])
        arrived(xt.at[:, cls, 2 * (1 - yl) + (1 - c)], cb_s.at[i], cb_r.at[i])
    total = jnp.zeros((ROWS, TOK), F32)
    for j in range(G):
        total += jnp.dot(
            w[:, j * 768 : (j + 1) * 768], xt[j].reshape(768, TOK), preferred_element_type=F32
        )
    proj[...] = dot_nt(eye(TOK), total.astype(BF16)).astype(BF16)
    x2[r] = xt[r]

    total = pf[q, g, s]
    for k in range(1, G):
        gg = (g + k) % G
        arrived(frecv.at[gg], rf_s.at[k], rf_r.at[gg])
        total += frecv[gg].astype(F32)
    cg[...] = dot_nt(eye(TOK), total.astype(BF16)).astype(BF16)

    for k in range(1, R):
        rr = (r + k) % R
        for y in range(2):
            arrived(x2.at[rr, :, 2 * y + 1 - c], xc_s.at[k, y], xc_r.at[k, y])
    grads = jnp.concatenate([oga[k] for k in range(R)], axis=1)
    for p in range(Q):
        columns = jnp.concatenate([x2[k, p].reshape(S * FB, TOK) for k in range(R)], axis=1)
        wg[:, p * S * FB : (p + 1) * S * FB] = dot_nt(grads, columns)

    for copy in pending:
        copy.wait_send()


def local(context, w_out, out_grad):
    vmem = pl.BlockSpec(memory_space=pltpu.VMEM)
    dma = pltpu.SemaphoreType.DMA
    return pl.pallas_call(
        kernel,
        out_shape=(
            jax.ShapeDtypeStruct((TOK, ROWS), BF16),
            jax.ShapeDtypeStruct((TOK, FB), BF16),
            jax.ShapeDtypeStruct((ROWS, Q * S * FB), F32),
        ),
        in_specs=[vmem] * 3,
        out_specs=(vmem,) * 3,
        scratch_shapes=[
            pltpu.VMEM((G, Q, S, FB, TOK), BF16),
            pltpu.VMEM((Q, G, S, FB, TOK), F32),
            pltpu.VMEM((Q, 2, G, FB, TOK), BF16),
            pltpu.VMEM((Q, 2, G, FB, TOK), BF16),
            pltpu.VMEM((Q, G, FB, TOK), BF16),
            pltpu.VMEM((Q, G, FB, TOK), BF16),
            pltpu.VMEM((3, G, FB, TOK), BF16),
            pltpu.VMEM((3, G, FB, TOK), BF16),
            pltpu.VMEM((G, FB, TOK), BF16),
            pltpu.VMEM((G, FB, TOK), BF16),
            pltpu.VMEM((R, ROWS, TOK), BF16),
            pltpu.VMEM((R, Q, S, FB, TOK), BF16),
            dma((G,)), dma((G,)), dma((4,)), dma((4,)), dma((Q,)), dma((Q,)), dma((Q,)), dma((Q,)),
            dma((Q,)), dma((Q,)), dma((R,)), dma((R,)), dma((R, 2)), dma((R, 2)), dma((R, 2)), dma((R, 2)),
            dma((Q,)), dma((Q,)), dma((Q,)), dma((Q,)), dma((4,)), dma((4,)), dma((G,)), dma((G,)),
        ],
        compiler_params=pltpu.CompilerParams(
            collective_id=0, has_side_effects=True, vmem_limit_bytes=40 * 2**20
        ),
        cost_estimate=pl.CostEstimate(
            flops=6 * TOK * ROWS * 6144, bytes_accessed=4_000_000, transcendentals=0
        ),
    )(context, w_out, out_grad)


def solution(mesh):
    placed = (P("dp", "tensor"), P("tensor", None), P("dp", "tensor"))
    return jax.shard_map(
        local,
        mesh=mesh,
        in_specs=placed,
        out_specs=(P("dp", "tensor"), P("dp", "tensor"), P("tensor", "dp")),
        check_vma=False,
    )
```

```python
import jax
import jax.numpy as jnp
from jax import lax
from jax.experimental import pallas as pl
from jax.experimental.pallas import tpu as pltpu
from jax.sharding import PartitionSpec as P

MESH = pl.DeviceIdType.MESH
F32, BF16 = jnp.float32, jnp.bfloat16
R, G, Q, S, FB, TOK, ROWS = 8, 8, 4, 4, 48, 128, 144


def dot_nt(a, b):
    return lax.dot_general(a, b, (((1,), (1,)), ((), ())), preferred_element_type=F32)


def eye(n):
    return (
        lax.broadcasted_iota(jnp.int32, (n, n), 0) == lax.broadcasted_iota(jnp.int32, (n, n), 1)
    ).astype(F32).astype(BF16)


def kernel(
    ctx, w, og, proj, cg, wg,
    xt, wv, pf, pc, rc, ysend, yrecv, nsend, nrecv, fsend, frecv, oga, x2, own_ctx, cg_half,
    ok, in_s, a_s, ns_s, x_s, b_s, xf_s, rc_s, ry_s, rn_s, rf_s, fa_s, og_s, one_s,
    fa_r, na_r, ya_r, ca_r, cb_r, og_r, x_r, xf_r, rc_r, ry_r, rn_r, rf_r, cx_r, cg_r,
):
    r = lax.axis_index("dp")
    t = lax.axis_index("tensor")
    z, s = t // 4, t % 4
    yl, c = s // 2, s % 2
    q, g = z % 4, z // 4
    sib = 2 * yl + (1 - c)
    par = 2 * (1 - yl) + c

    def at(gp, qp):
        return (r, (4 * gp + qp) * 4 + s)

    def at_z(zz):
        return (r, zz * 4 + s)

    near = [(q + d) % 4 for d in range(4)]
    core_dev, y_dev = (r, z * 4 + sib), (r, z * 4 + par)

    loads = [
        pltpu.make_async_copy(og, oga.at[r], in_s.at[0]),
        pltpu.make_async_copy(w, wv, in_s.at[1]),
        pltpu.make_async_copy(ctx, own_ctx, in_s.at[2]),
    ]
    for load in loads:
        load.start()

    def greet(semaphore, device):
        pl.semaphore_signal(semaphore, inc=1, device_id=device, device_id_type=MESH)

    rank = jnp.where(g < 4, g, 11 - g)

    def above(gp):
        return (gp if gp < 4 else 11 - gp) > rank

    def below(gp):
        return (gp if gp < 4 else 11 - gp) < rank

    def beside(gp):
        return ((gp - g + 8) % 8 == 1) | ((gp - g + 8) % 8 == 7)

    def meets(gp):
        return beside(gp) | ((c == 0) & ((g < 4) != (gp < 4)))

    def number(condition):
        return jnp.where(condition, 1, 0)

    ends = (z == 0) | (z == 3) | (z == 28) | (z == 31)
    facing = jnp.where((z == 0) | (z == 28), z + 3, jnp.where(ends, z - 3, z))
    expected = number(ends)
    barrier = pltpu.get_barrier_semaphore()
    for d in (1, -1, 2, -2):

        @pl.when((z + d >= 0) & (z + d < 32))
        def _():
            greet(barrier, at_z(z + d))

        expected += number((z + d >= 0) & (z + d < 32))

    @pl.when(ends)
    def _():
        greet(barrier, at_z(facing))

    partners = [core_dev, y_dev]
    for k in range(1, R):
        partners += [((r + k) % R, z * 4 + sp) for sp in ((s, par) if k % 2 else (s,))]
    for gp in range(G):

        @pl.when(above(gp) & meets(gp))
        def _():
            greet(barrier, at(gp, q))

        expected += number(below(gp) & meets(gp))
    for device in partners:
        greet(barrier, device)

    loads[0].wait()
    grad = dot_nt(eye(TOK), oga[r]).astype(BF16)
    loads[1].wait()
    for j in range(16):
        part = jnp.dot(grad, wv[:, j * 384 : (j + 1) * 384], preferred_element_type=F32)
        part = part.T.reshape(2, 2, 2, FB, TOK)
        for i in range(2):
            zz = 2 * j + i
            pf[zz % 4, zz // 4] = part[i]
    order = (2, 1, 3, 0)

    @pl.when(c == 0)
    def _():
        for d in order:
            pc[near[d]] = pf[near[d]].astype(BF16)

    loads[2].wait()
    pl.semaphore_wait(barrier, len(partners) + expected)

    def copy_of(src, dst, ssem, rsem, device):
        return pltpu.make_async_remote_copy(
            src_ref=src, dst_ref=dst, send_sem=ssem, recv_sem=rsem, device_id=device, device_id_type=MESH
        )

    def send(src, dst, ssem, rsem, device):
        copy_of(src, dst, ssem, rsem, device).start()

    def arrived(dst, rsem):
        copy_of(dst, dst, rsem, rsem, core_dev).wait_recv()

    def sent(all_of_it, ssem):
        copy_of(all_of_it, all_of_it, ssem, ssem, core_dev).wait_send()

    def share_grads():
        for k in range(1, R):
            send(oga.at[r], oga.at[r], og_s, og_r, ((r + k) % R, t))

    def half(h):
        return pl.ds(4 * h, 4)

    def straight(b, gp):
        return (b >= 4) & (gp < 4)

    def hop(k, step, act):
        b, target = (g - step * k + 8) % 8, (g + step + 8) % 8
        block = xt.at[b, q, yl]

        @pl.when(jnp.logical_not(straight(b, target)))
        def _():
            act(copy_of(block, block, fa_s.at[k if step == 1 else 4 + k], fa_r.at[b], at(target, q)))

    def jump(gp, act):
        block = xt.at[g, q, yl]

        @pl.when(g >= 4)
        def _():
            act(copy_of(block, block, fa_s.at[7 + gp], fa_r.at[g], at(gp, q)))

    def start(copy):
        copy.start()

    def wait_sent(copy):
        copy.wait_send()

    def rounds(wanted):
        for k, step in ((1, 1), (1, -1), (2, 1), (2, -1), (3, 1), (3, -1), (4, 1)):
            b = (g - step * k + 8) % 8

            @pl.when(wanted(b))
            def _():
                arrived(xt.at[b, q, yl], fa_r.at[b])
                if k < (4 if step == 1 else 3):
                    hop(k, step, start)

    def spread(d, h):
        mine = xt.at[half(h), near[d], yl]
        send(mine, mine, a_s, ya_r.at[d, h], y_dev)

    def near_sends(h, act):
        own = xt.at[half(h), q, yl]
        way = 2 if h == 0 else -2
        for i, slot, when, target in (
            (0, 2, (z + way >= 0) & (z + way < 32), z + way),
            (1, 0, z < 31, z + 1),
            (2, 1, z > 0, z - 1),
            (3, 0, z == 3, z - 3),
            (4, 1, z == 28, z + 3),
            (5, 2, (z == 2) | (z == 3) if h == 0 else (z == 28) | (z == 29), z - way),
        ):

            @pl.when(when)
            def _():
                act(copy_of(own, own, ns_s.at[i, h], na_r.at[slot, h], at_z(target)))

    def far_done(h):
        near_sends(h, start)
        spread(0, h)

    def near_arrived(h):
        for d, slot in ((3, 0), (1, 1), (2, 2)):
            arrived(xt.at[half(h), near[d], yl], na_r.at[slot, h])
            spread(d, h)
        mine = xt.at[half(h), :, yl]
        send(mine, mine, b_s, ca_r.at[h], core_dev)

    def pair_arrived(d, h):
        arrived(xt.at[half(h), near[d], 1 - yl], ya_r.at[d, h])
        for rr in range(4 * h, 4 * h + 4):

            @pl.when(rr != r)
            def _():
                target = (rr, z * 4 + jnp.where((rr - r + 8) % 2 == 0, s, par))
                send(xt.at[rr, near[d]], x2.at[r, near[d]], x_s, x_r.at[r], target)

    def pair_done(h):
        for d in (3, 1, 2):
            pair_arrived(d, h)
        theirs = xt.at[half(h), :, 1 - yl]
        send(theirs, theirs, b_s, cb_r.at[h], core_dev)

    def project():
        total = jnp.zeros((ROWS, TOK), F32)
        for j in range(G):
            total += jnp.dot(
                wv[:, j * 768 : (j + 1) * 768], xt[j].reshape(768, TOK), preferred_element_type=F32
            )
        proj[...] = total.astype(BF16)
        x2[r] = xt[r]

    def weight_grads():
        grads = jnp.concatenate([oga[k] for k in range(R)], axis=1)
        for p in range(Q):
            columns = jnp.concatenate([x2[k, p].reshape(S * FB, TOK) for k in range(R)], axis=1)
            wg[:, p * S * FB : (p + 1) * S * FB] = dot_nt(grads, columns)

    @pl.when(c == 0)
    def _():
        xt[g, q, yl, 0] = own_ctx[...]

    def answer():
        for gp in range(G):

            @pl.when(below(gp) & beside(gp))
            def _():
                greet(ok.at[g], at(gp, q))

    def admitted(step):
        for gp in range(G):

            @pl.when(above(gp) & ((gp - g + 8) % 8 == step % 8))
            def _():
                pl.semaphore_wait(ok.at[gp], 1)

    @pl.when(c == 0)
    def _():
        answer()
        for i, d in enumerate(order):
            send(pc.at[near[d]], rc.at[near[d]], rc_s, rc_r.at[i], core_dev)
        arrived(xt.at[g, q, yl, 1], cx_r)
        for gp in range(4):
            jump(gp, start)

        def first_hop(step):
            admitted(step)
            hop(0, step, start)

        @pl.when(g == 0)
        def _():
            first_hop(1)

        first_hop(-1)

        @pl.when(g > 0)
        def _():
            first_hop(1)

        share_grads()

        @pl.when(g < 4)
        def _():
            rounds(lambda b: b < 4)
            far_done(0)
            rounds(lambda b: b >= 4)
            far_done(1)

        @pl.when(g >= 4)
        def _():
            rounds(lambda b: b != (g + 4) % 8)
            far_done(1)
            rounds(lambda b: b == (g + 4) % 8)
            far_done(0)

        pair_arrived(0, 0)
        near_arrived(0)
        pair_arrived(0, 1)
        near_arrived(1)
        pair_done(0)
        pair_done(1)
        for k in range(1, R):
            rr = (r + k) % R
            arrived(x2.at[rr], x_r.at[rr])
            send(x2.at[rr], x2.at[rr], xf_s, xf_r, core_dev)
        project()
        arrived(oga.at[0:7], og_r)
        weight_grads()
        arrived(cg_half, cg_r)
        cg[...] = cg_half[...]
        for k in range(4):
            hop(k, 1, wait_sent)
        for k in range(3):
            hop(k, -1, wait_sent)
        for gp in range(4):
            jump(gp, wait_sent)
        for h in range(2):
            near_sends(h, wait_sent)
        sent(x2.at[0:4], a_s)
        sent(x2.at[0:7], x_s)
        sent(x2, b_s)
        sent(x2.at[0:7], xf_s)
        sent(pc, rc_s)
        sent(oga.at[0:7], og_s)

    @pl.when(c == 1)
    def _():
        send(own_ctx, xt.at[g, q, yl, 1], one_s.at[0], cx_r, core_dev)
        answer()
        share_grads()
        for i, d in enumerate(order):
            cls = near[d]
            arrived(rc.at[cls], rc_r.at[i])
            ysend[cls] = (pf[cls, :, 1 - yl] + rc[cls, :, 1 - yl].astype(F32)).astype(BF16)
            send(ysend.at[cls], yrecv.at[cls], ry_s, ry_r.at[i], y_dev)
        for i, d in enumerate(order):
            cls = near[d]
            arrived(yrecv.at[cls], ry_r.at[i])
            total = pf[cls, :, yl] + rc[cls, :, yl].astype(F32) + yrecv[cls].astype(F32)
            if d == 0:
                pf[cls, :, yl] = total
            else:
                nsend[d - 1] = total.astype(BF16)
                if d == 2:
                    i0, i1 = jnp.where(z < 2, 4, 2), jnp.where(z > 29, 4, 2)
                    send(nsend.at[1, 0:4], nrecv.at[i0, 0:4], rn_s, rn_r.at[i0], at_z(jnp.where(z < 2, z + 2, z - 2)))
                    i2 = jnp.where(z > 29, 4, 5)
                    send(nsend.at[1, 4:8], nrecv.at[i1, 4:8], rn_s, rn_r.at[i2], at_z(jnp.where(z > 29, z - 2, z + 2)))
                elif d == 1:
                    i0 = jnp.where(z == 31, 3, 1)
                    send(nsend.at[0], nrecv.at[i0], rn_s, rn_r.at[i0], at_z(jnp.where(z == 31, z - 3, z + 1)))
                else:
                    i0 = jnp.where(z == 0, 3, 0)
                    send(nsend.at[2], nrecv.at[i0], rn_s, rn_r.at[i0], at_z(jnp.where(z == 0, z + 3, z - 1)))
        for here, ref, sem in (
            (z < 31, nrecv.at[0], 0),
            (z > 0, nrecv.at[1], 1),
            (z < 30, nrecv.at[2, 0:4], 2),
            (z > 1, nrecv.at[2, 4:8], 5),
        ):

            @pl.when(here)
            def _():
                arrived(ref, rn_r.at[sem])

            @pl.when(jnp.logical_not(here))
            def _():
                ref[...] = jnp.zeros(ref.shape, BF16)

        window = pf[q, :, yl] + nrecv[0].astype(F32) + nrecv[1].astype(F32) + nrecv[2].astype(F32)
        pf[q, :, yl] = window
        for here, ref, sem, low, high in (
            ((z == 3) | (z == 28), nrecv.at[3], 3, 0, 8),
            ((z == 2) | (z == 3), nrecv.at[4, 0:4], 4, 0, 4),
            ((z == 28) | (z == 29), nrecv.at[4, 4:8], 4, 4, 8),
        ):

            @pl.when(here)
            def _():
                arrived(ref, rn_r.at[sem])
                pf[q, low:high, yl] += ref[...].astype(F32)

        admitted(1)
        admitted(-1)
        for k, step in ((1, 1), (1, -1), (2, 1), (2, -1), (3, 1), (3, -1), (4, 1)):
            last = 4 if step == 1 else 3
            slot = k - 1 if step == 1 else 3 + k
            partial = pf[q, (g + step * (last + 1 - k) + 8) % 8, yl]
            if k > 1:
                arrived(frecv.at[slot - 1], rf_r.at[slot - 1])
                partial += frecv[slot - 1].astype(F32)
            fsend[slot] = partial.astype(BF16)
            send(fsend.at[slot], frecv.at[slot], rf_s, rf_r.at[slot], at((g + step + 8) % 8, q))
        total = pf[q, g, yl]
        for slot in (6, 3):
            arrived(frecv.at[slot], rf_r.at[slot])
            total += frecv[slot].astype(F32)
        total = total.astype(BF16)
        sent(own_ctx, one_s.at[0])
        cg_half[...] = total[0]
        send(cg_half, cg_half, one_s.at[1], cg_r, core_dev)
        cg[...] = total[1]
        for h in range(2):
            arrived(xt.at[half(h), :, yl], ca_r.at[h])
            arrived(xt.at[half(h), :, 1 - yl], cb_r.at[h])
        project()
        arrived(oga.at[0:7], og_r)
        arrived(x2.at[0:7], xf_r)
        weight_grads()
        sent(cg_half, one_s.at[1])
        sent(ysend, ry_s)
        sent(nsend, rn_s)
        sent(fsend, rf_s)
        sent(oga.at[0:7], og_s)


def local(context, w_out, out_grad):
    vmem = pl.BlockSpec(memory_space=pltpu.VMEM)
    dma = pltpu.SemaphoreType.DMA
    projected, context_grad, weight_grad = pl.pallas_call(
        kernel,
        out_shape=(
            jax.ShapeDtypeStruct((ROWS, TOK), BF16),
            jax.ShapeDtypeStruct((FB, TOK), BF16),
            jax.ShapeDtypeStruct((ROWS, Q * S * FB), F32),
        ),
        in_specs=[pl.BlockSpec(memory_space=pltpu.HBM)] * 3,
        out_specs=(vmem,) * 3,
        scratch_shapes=[
            pltpu.VMEM((G, Q, 2, 2, FB, TOK), BF16),
            pltpu.VMEM((ROWS, G * Q * S * FB), BF16),
            pltpu.VMEM((Q, G, 2, 2, FB, TOK), F32),
            pltpu.VMEM((Q, G, 2, 2, FB, TOK), BF16),
            pltpu.VMEM((Q, G, 2, 2, FB, TOK), BF16),
            pltpu.VMEM((Q, G, 2, FB, TOK), BF16),
            pltpu.VMEM((Q, G, 2, FB, TOK), BF16),
            pltpu.VMEM((3, G, 2, FB, TOK), BF16),
            pltpu.VMEM((5, G, 2, FB, TOK), BF16),
            pltpu.VMEM((7, 2, FB, TOK), BF16),
            pltpu.VMEM((7, 2, FB, TOK), BF16),
            pltpu.VMEM((R, ROWS, TOK), BF16),
            pltpu.VMEM((R, Q, 2, 2, FB, TOK), BF16),
            pltpu.VMEM((FB, TOK), BF16),
            pltpu.VMEM((FB, TOK), BF16),
            pltpu.SemaphoreType.REGULAR((G,)), dma((3,)),
            dma, dma((6, 2)), dma, dma, dma, dma, dma, dma, dma, dma((11,)), dma, dma((2,)),
            dma((G,)), dma((3, 2)), dma((Q, 2)), dma((2,)), dma((2,)), dma, dma((R,)), dma, dma((Q,)), dma((Q,)),
            dma((6,)), dma((7,)), dma, dma,
        ],
        compiler_params=pltpu.CompilerParams(
            collective_id=0, has_side_effects=True, vmem_limit_bytes=52 * 2**20
        ),
        cost_estimate=pl.CostEstimate(
            flops=6 * TOK * ROWS * 6144, bytes_accessed=4_000_000, transcendentals=0
        ),
    )(context.T, w_out, out_grad.T)
    return projected.T, context_grad.T, weight_grad


def solution(mesh):
    placed = (P("dp", "tensor"), P("tensor", None), P("dp", "tensor"))
    return jax.shard_map(
        local,
        mesh=mesh,
        in_specs=placed,
        out_specs=(P("dp", "tensor"), P("dp", "tensor"), P("tensor", "dp")),
        check_vma=False,
    )
```

```python
import jax
import jax.numpy as jnp
from jax import lax
from jax.experimental import pallas as pl
from jax.experimental.pallas import tpu as pltpu
from jax.sharding import PartitionSpec as P

MESH = pl.DeviceIdType.MESH
F32, BF16 = jnp.float32, jnp.bfloat16
R, G, Q, S, FB, TOK, ROWS = 8, 8, 4, 4, 48, 128, 144


def dot_nt(a, b):
    return lax.dot_general(a, b, (((1,), (1,)), ((), ())), preferred_element_type=F32)


def eye(n):
    return (
        lax.broadcasted_iota(jnp.int32, (n, n), 0) == lax.broadcasted_iota(jnp.int32, (n, n), 1)
    ).astype(F32).astype(BF16)


def kernel(
    ctx, w, og, proj, cg, wg,
    xt, wv, pf, pc, rc, ysend, yrecv, nsend, nrecv, fsend, frecv, oga, x2, own_ctx, cg_half,
    ok, in_s, a_s, ns_s, x_s, b_s, xf_s, rc_s, ry_s, rn_s, rf_s, fa_s, og_s, one_s,
    fa_r, na_r, ya_r, ca_r, cb_r, og_r, x_r, xf_r, rc_r, ry_r, rn_r, rf_r, cx_r, cg_r,
):
    r = lax.axis_index("dp")
    t = lax.axis_index("tensor")
    z, s = t // 4, t % 4
    yl, c = s // 2, s % 2
    q, g = z % 4, z // 4
    sib = 2 * yl + (1 - c)
    par = 2 * (1 - yl) + c
    oth = 2 * (1 - yl) + (1 - c)

    def at(gp, qp):
        return (r, (4 * gp + qp) * 4 + s)

    def at_z(zz):
        return (r, zz * 4 + s)

    near = [(q + d) % 4 for d in range(4)]
    core_dev, y_dev = (r, z * 4 + sib), (r, z * 4 + par)

    loads = [
        pltpu.make_async_copy(og, oga.at[r], in_s.at[0]),
        pltpu.make_async_copy(w, wv, in_s.at[1]),
        pltpu.make_async_copy(ctx, own_ctx, in_s.at[2]),
    ]
    for load in loads:
        load.start()

    def greet(semaphore, device):
        pl.semaphore_signal(semaphore, inc=1, device_id=device, device_id_type=MESH)

    rank = jnp.where(g < 4, g, 11 - g)

    def above(gp):
        return (gp if gp < 4 else 11 - gp) > rank

    def below(gp):
        return (gp if gp < 4 else 11 - gp) < rank

    def beside(gp):
        return ((gp - g + 8) % 8 == 1) | ((gp - g + 8) % 8 == 7)

    def straight(b, gp):
        return ((b >= 4) & (gp < 3)) | ((b == 3) & (gp == 0))

    def meets(gp):
        return beside(gp) | straight(g, gp) | straight(gp, g)

    def number(condition):
        return jnp.where(condition, 1, 0)

    ends = (z == 0) | (z == 3) | (z == 28) | (z == 31)
    facing = jnp.where((z == 0) | (z == 28), z + 3, jnp.where(ends, z - 3, z))
    expected = number(ends)
    barrier = pltpu.get_barrier_semaphore()
    for d in (1, -1, 2, -2):

        @pl.when((z + d >= 0) & (z + d < 32))
        def _():
            greet(barrier, at_z(z + d))

        expected += number((z + d >= 0) & (z + d < 32))

    @pl.when(ends)
    def _():
        greet(barrier, at_z(facing))

    partners = [core_dev, y_dev]
    for k in range(1, R):
        partners += [((r + k) % R, z * 4 + sp) for sp in ((s, par, oth) if k % 2 else (s, sib))]
    for gp in range(G):

        @pl.when(above(gp) & meets(gp))
        def _():
            greet(barrier, at(gp, q))

        expected += number(below(gp) & meets(gp))
    for device in partners:
        greet(barrier, device)

    loads[0].wait()
    grad = dot_nt(eye(TOK), oga[r]).astype(BF16)
    loads[1].wait()
    for j in range(16):
        part = jnp.dot(grad, wv[:, j * 384 : (j + 1) * 384], preferred_element_type=F32)
        part = part.T.reshape(2, 2, 2, FB, TOK)
        for i in range(2):
            zz = 2 * j + i
            pf[zz % 4, zz // 4] = part[i]
    order = (2, 1, 3, 0)

    @pl.when(c == 0)
    def _():
        for d in order:
            pc[near[d]] = pf[near[d]].astype(BF16)

    loads[2].wait()
    pl.semaphore_wait(barrier, len(partners) + expected)

    def copy_of(src, dst, ssem, rsem, device):
        return pltpu.make_async_remote_copy(
            src_ref=src, dst_ref=dst, send_sem=ssem, recv_sem=rsem, device_id=device, device_id_type=MESH
        )

    def send(src, dst, ssem, rsem, device):
        copy_of(src, dst, ssem, rsem, device).start()

    def arrived(dst, rsem):
        copy_of(dst, dst, rsem, rsem, core_dev).wait_recv()

    def sent(all_of_it, ssem):
        copy_of(all_of_it, all_of_it, ssem, ssem, core_dev).wait_send()

    def share_grads():
        for k in range(1, R):
            send(oga.at[r], oga.at[r], og_s, og_r, ((r + k) % R, t))

    def half(h):
        return pl.ds(4 * h, 4)

    def hop(k, step, act):
        b, target = (g - step * k + 8) % 8, (g + step + 8) % 8
        block = xt.at[b, q, yl]

        goes = jnp.logical_not(straight(b, target))
        if k == 3:
            goes = (b < 2) if step == 1 else ((b == 2) | (b == 3) | (b == 7))

        @pl.when(goes)
        def _():
            act(copy_of(block, block, fa_s.at[k if step == 1 else 4 + k], fa_r.at[b], at(target, q)))

    def jump(gp, act):
        block = xt.at[g, q, yl]

        @pl.when(straight(g, gp))
        def _():
            act(copy_of(block, block, fa_s.at[8 + gp], fa_r.at[g], at(gp, q)))

    def start(copy):
        copy.start()

    def wait_sent(copy):
        copy.wait_send()

    def rounds(wanted):
        for k, step in ((1, 1), (1, -1), (2, 1), (2, -1), (3, 1), (3, -1), (4, 1)):
            b = (g - step * k + 8) % 8

            @pl.when(wanted(b))
            def _():
                arrived(xt.at[b, q, yl], fa_r.at[b])
                if k < 4:
                    hop(k, step, start)

    held = ((0, 3), (1, 2))

    def spread(d, h):
        mine = xt.at[half(h), near[d], yl]
        send(mine, mine, a_s, ya_r.at[d, h], y_dev)

    def near_sends(h, act):
        own = xt.at[half(h), q, yl]
        way = 2 if h == 0 else -2
        for i, slot, when, target in (
            (0, 2, (z + way >= 0) & (z + way < 32), z + way),
            (1, 0, z < 31, z + 1),
            (2, 1, z > 0, z - 1),
            (3, 0, z == 3, z - 3),
            (4, 1, z == 28, z + 3),
            (5, 2, (z == 2) | (z == 3) if h == 0 else (z == 28) | (z == 29), z - way),
        ):

            @pl.when(when)
            def _():
                act(copy_of(own, own, ns_s.at[i, h], na_r.at[slot, h], at_z(target)))

    def far_done(h):
        near_sends(h, start)
        spread(0, h)

    def near_arrived(h):
        for d, slot in ((3, 0), (1, 1), (2, 2)):
            arrived(xt.at[half(h), near[d], yl], na_r.at[slot, h])
            spread(d, h)
        mine = xt.at[half(h), :, yl]
        send(mine, mine, b_s, ca_r.at[h], core_dev)

    def pair_arrived(d, h):
        arrived(xt.at[half(h), near[d], 1 - yl], ya_r.at[d, h])
        for rr in range(4 * h, 4 * h + 4):

            @pl.when(rr != r)
            def _():
                ours, others = (s, par) if d in held[0] else (sib, oth)
                target = (rr, z * 4 + jnp.where((rr - r + 8) % 2 == 0, ours, others))
                send(xt.at[rr, near[d]], x2.at[r, near[d]], x_s, x_r.at[r], target)

    def pair_done(h):
        for d in (3, 1, 2):
            pair_arrived(d, h)
        theirs = xt.at[half(h), :, 1 - yl]
        send(theirs, theirs, b_s, cb_r.at[h], core_dev)

    def exchange(mine):
        for k in range(1, R):
            rr = (r + k) % R
            arrived(x2.at[rr, 0:2], x_r.at[rr])
            for d in mine:
                piece = x2.at[rr, near[d]]
                send(piece, piece, xf_s, xf_r, core_dev)

    def project():
        total = jnp.zeros((ROWS, TOK), F32)
        for j in range(G):
            total += jnp.dot(
                wv[:, j * 768 : (j + 1) * 768], xt[j].reshape(768, TOK), preferred_element_type=F32
            )
        proj[...] = total.astype(BF16)
        x2[r] = xt[r]

    def weight_grads():
        grads = jnp.concatenate([oga[k] for k in range(R)], axis=1)
        for p in range(Q):
            columns = jnp.concatenate([x2[k, p].reshape(S * FB, TOK) for k in range(R)], axis=1)
            wg[:, p * S * FB : (p + 1) * S * FB] = dot_nt(grads, columns)

    @pl.when(c == 0)
    def _():
        xt[g, q, yl, 0] = own_ctx[...]

    def answer():
        for gp in range(G):

            @pl.when(below(gp) & beside(gp))
            def _():
                greet(ok.at[g], at(gp, q))

    def admitted(step):
        for gp in range(G):

            @pl.when(above(gp) & ((gp - g + 8) % 8 == step % 8))
            def _():
                pl.semaphore_wait(ok.at[gp], 1)

    @pl.when(c == 0)
    def _():
        answer()
        for i, d in enumerate(order):
            send(pc.at[near[d]], rc.at[near[d]], rc_s, rc_r.at[i], core_dev)
        arrived(xt.at[g, q, yl, 1], cx_r)
        for gp in range(3):
            jump(gp, start)

        def first_hop(step):
            admitted(step)
            hop(0, step, start)

        @pl.when(g == 0)
        def _():
            first_hop(1)

        first_hop(-1)

        @pl.when(g > 0)
        def _():
            first_hop(1)

        share_grads()

        @pl.when(g < 4)
        def _():
            rounds(lambda b: b < 4)
            far_done(0)
            rounds(lambda b: b >= 4)
            far_done(1)

        @pl.when(g >= 4)
        def _():
            rounds(lambda b: b != (g + 4) % 8)
            far_done(1)
            rounds(lambda b: b == (g + 4) % 8)
            far_done(0)

        pair_arrived(0, 0)
        near_arrived(0)
        pair_arrived(0, 1)
        near_arrived(1)
        pair_done(0)
        pair_done(1)
        exchange(held[0])
        project()
        arrived(oga.at[0:7], og_r)
        arrived(x2.at[0:7, 0:2], xf_r)
        weight_grads()
        arrived(cg_half, cg_r)
        cg[...] = cg_half[...]
        for k in range(4):
            hop(k, 1, wait_sent)
            hop(k, -1, wait_sent)
        for gp in range(3):
            jump(gp, wait_sent)
        for h in range(2):
            near_sends(h, wait_sent)
        sent(x2.at[0:4], a_s)
        sent(x2.at[0:7], x_s)
        sent(x2, b_s)
        sent(x2.at[0:7, 0:2], xf_s)
        sent(pc, rc_s)
        sent(oga.at[0:7], og_s)

    legs = ((1, 1), (1, -1), (2, 1), (2, -1), (3, 1), (3, -1), (4, 1))

    def leg(k, step):
        last = 4 if step == 1 else 3
        target = (g + step * (last + 1 - k) + 8) % 8
        goes = (target > 2) | (g < 4)
        fed = (target > 2) | ((g - step >= 0) & (g - step < 4))
        return (k - 1 if step == 1 else 3 + k), target, goes, fed

    def rs_copy(slot, there, device):
        return copy_of(fsend.at[slot], frecv.at[there], rf_s.at[slot], rf_r.at[there], device)

    @pl.when(c == 1)
    def _():
        send(own_ctx, xt.at[g, q, yl, 1], one_s.at[0], cx_r, core_dev)
        answer()
        share_grads()
        for i, d in enumerate(order):
            cls = near[d]
            arrived(rc.at[cls], rc_r.at[i])
            ysend[cls] = (pf[cls, :, 1 - yl] + rc[cls, :, 1 - yl].astype(F32)).astype(BF16)
            send(ysend.at[cls], yrecv.at[cls], ry_s, ry_r.at[i], y_dev)
        for i, d in enumerate(order):
            cls = near[d]
            arrived(yrecv.at[cls], ry_r.at[i])
            total = pf[cls, :, yl] + rc[cls, :, yl].astype(F32) + yrecv[cls].astype(F32)
            if d == 0:
                pf[cls, :, yl] = total
            else:
                nsend[d - 1] = total.astype(BF16)
                if d == 2:
                    i0, i1 = jnp.where(z < 2, 4, 2), jnp.where(z > 29, 4, 2)
                    send(nsend.at[1, 0:4], nrecv.at[i0, 0:4], rn_s, rn_r.at[i0], at_z(jnp.where(z < 2, z + 2, z - 2)))
                    i2 = jnp.where(z > 29, 4, 5)
                    send(nsend.at[1, 4:8], nrecv.at[i1, 4:8], rn_s, rn_r.at[i2], at_z(jnp.where(z > 29, z - 2, z + 2)))
                elif d == 1:
                    i0 = jnp.where(z == 31, 3, 1)
                    send(nsend.at[0], nrecv.at[i0], rn_s, rn_r.at[i0], at_z(jnp.where(z == 31, z - 3, z + 1)))
                else:
                    i0 = jnp.where(z == 0, 3, 0)
                    send(nsend.at[2], nrecv.at[i0], rn_s, rn_r.at[i0], at_z(jnp.where(z == 0, z + 3, z - 1)))
        for here, ref, sem in (
            (z < 31, nrecv.at[0], 0),
            (z > 0, nrecv.at[1], 1),
            (z < 30, nrecv.at[2, 0:4], 2),
            (z > 1, nrecv.at[2, 4:8], 5),
        ):

            @pl.when(here)
            def _():
                arrived(ref, rn_r.at[sem])

            @pl.when(jnp.logical_not(here))
            def _():
                ref[...] = jnp.zeros(ref.shape, BF16)

        window = pf[q, :, yl] + nrecv[0].astype(F32) + nrecv[1].astype(F32) + nrecv[2].astype(F32)
        pf[q, :, yl] = window
        for here, ref, sem, low, high in (
            ((z == 3) | (z == 28), nrecv.at[3], 3, 0, 8),
            ((z == 2) | (z == 3), nrecv.at[4, 0:4], 4, 0, 4),
            ((z == 28) | (z == 29), nrecv.at[4, 4:8], 4, 4, 8),
        ):

            @pl.when(here)
            def _():
                arrived(ref, rn_r.at[sem])
                pf[q, low:high, yl] += ref[...].astype(F32)

        admitted(1)
        admitted(-1)
        for gp in range(3):

            @pl.when(g >= 4)
            def _():
                fsend[7 + gp] = pf[q, gp, yl].astype(BF16)
                rs_copy(7 + gp, 3 + g, at(gp, q)).start()

        def pass_on(k, step, early):
            slot, target, goes, fed = leg(k, step)
            goes = goes & early(target)

            @pl.when(goes)
            def _():
                fsend[slot] = pf[q, target, yl].astype(BF16)

            if k > 1:

                @pl.when(goes & fed)
                def _():
                    arrived(frecv.at[slot - 1], rf_r.at[slot - 1])
                    fsend[slot] = (pf[q, target, yl] + frecv[slot - 1].astype(F32)).astype(BF16)

            @pl.when(goes)
            def _():
                rs_copy(slot, slot, at((g + step + 8) % 8, q)).start()

        for k, step in legs[:2]:
            pass_on(k, step, lambda target: target >= 0)
        for k, step in legs[2:]:
            pass_on(k, step, lambda target: target < 3)
        for k, step in legs[2:]:
            pass_on(k, step, lambda target: target >= 3)

        for h in range(2):
            arrived(xt.at[half(h), :, yl], ca_r.at[h])
            arrived(xt.at[half(h), :, 1 - yl], cb_r.at[h])
        project()
        exchange(held[1])

        for slot, here in [(6, g >= 0), (3, g != 0)] + [(b + 3, g < 3) for b in range(4, 8)]:

            @pl.when(here)
            def _():
                arrived(frecv.at[slot], rf_r.at[slot])
                pf[q, g, yl] += frecv[slot].astype(F32)

        total = pf[q, g, yl].astype(BF16)
        sent(own_ctx, one_s.at[0])
        cg_half[...] = total[0]
        send(cg_half, cg_half, one_s.at[1], cg_r, core_dev)
        cg[...] = total[1]
        arrived(oga.at[0:7], og_r)
        arrived(x2.at[0:7, 0:2], xf_r)
        weight_grads()
        for gp in range(3):

            @pl.when(g >= 4)
            def _():
                rs_copy(7 + gp, 3 + g, at(gp, q)).wait_send()

        for k, step in legs:
            slot, target, goes, fed = leg(k, step)

            @pl.when(goes)
            def _():
                rs_copy(slot, slot, at((g + step + 8) % 8, q)).wait_send()

        sent(x2.at[0:7, 0:2], xf_s)
        sent(cg_half, one_s.at[1])
        sent(ysend, ry_s)
        sent(nsend, rn_s)
        sent(oga.at[0:7], og_s)


def local(context, w_out, out_grad):
    vmem = pl.BlockSpec(memory_space=pltpu.VMEM)
    dma = pltpu.SemaphoreType.DMA
    projected, context_grad, weight_grad = pl.pallas_call(
        kernel,
        out_shape=(
            jax.ShapeDtypeStruct((ROWS, TOK), BF16),
            jax.ShapeDtypeStruct((FB, TOK), BF16),
            jax.ShapeDtypeStruct((ROWS, Q * S * FB), F32),
        ),
        in_specs=[pl.BlockSpec(memory_space=pltpu.HBM)] * 3,
        out_specs=(vmem,) * 3,
        scratch_shapes=[
            pltpu.VMEM((G, Q, 2, 2, FB, TOK), BF16),
            pltpu.VMEM((ROWS, G * Q * S * FB), BF16),
            pltpu.VMEM((Q, G, 2, 2, FB, TOK), F32),
            pltpu.VMEM((Q, G, 2, 2, FB, TOK), BF16),
            pltpu.VMEM((Q, G, 2, 2, FB, TOK), BF16),
            pltpu.VMEM((Q, G, 2, FB, TOK), BF16),
            pltpu.VMEM((Q, G, 2, FB, TOK), BF16),
            pltpu.VMEM((3, G, 2, FB, TOK), BF16),
            pltpu.VMEM((5, G, 2, FB, TOK), BF16),
            pltpu.VMEM((10, 2, FB, TOK), BF16),
            pltpu.VMEM((11, 2, FB, TOK), BF16),
            pltpu.VMEM((R, ROWS, TOK), BF16),
            pltpu.VMEM((R, Q, 2, 2, FB, TOK), BF16),
            pltpu.VMEM((FB, TOK), BF16),
            pltpu.VMEM((FB, TOK), BF16),
            pltpu.SemaphoreType.REGULAR((G,)), dma((3,)),
            dma, dma((6, 2)), dma, dma, dma, dma, dma, dma, dma((10,)), dma((11,)), dma, dma((2,)),
            dma((G,)), dma((3, 2)), dma((Q, 2)), dma((2,)), dma((2,)), dma, dma((R,)), dma, dma((Q,)), dma((Q,)),
            dma((6,)), dma((11,)), dma, dma,
        ],
        compiler_params=pltpu.CompilerParams(
            collective_id=0, has_side_effects=True, vmem_limit_bytes=52 * 2**20
        ),
        cost_estimate=pl.CostEstimate(
            flops=6 * TOK * ROWS * 6144, bytes_accessed=4_000_000, transcendentals=0
        ),
    )(context.T, w_out, out_grad.T)
    return projected.T, context_grad.T, weight_grad


def solution(mesh):
    placed = (P("dp", "tensor"), P("tensor", None), P("dp", "tensor"))
    return jax.shard_map(
        local,
        mesh=mesh,
        in_specs=placed,
        out_specs=(P("dp", "tensor"), P("dp", "tensor"), P("tensor", "dp")),
        check_vma=False,
    )
```

```python
import jax
import jax.numpy as jnp
from jax import lax
from jax.experimental import pallas as pl
from jax.experimental.pallas import tpu as pltpu
from jax.sharding import PartitionSpec as P

MESH = pl.DeviceIdType.MESH
F32, BF16 = jnp.float32, jnp.bfloat16
R, G, Q, S, FB, TOK, ROWS = 8, 8, 4, 4, 48, 128, 144


def dot_nt(a, b):
    return lax.dot_general(a, b, (((1,), (1,)), ((), ())), preferred_element_type=F32)


def eye(n):
    return (
        lax.broadcasted_iota(jnp.int32, (n, n), 0) == lax.broadcasted_iota(jnp.int32, (n, n), 1)
    ).astype(F32).astype(BF16)


def kernel(
    ctx, w, og, proj, cg, wg,
    xt, wv, pf, pc, rc, ysend, yrecv, nsend, nrecv, fsend, frecv, oga, x2, own_ctx, cg_half, ogx, wgp, wgx,
    ok, in_s, a_s, ns_s, x_s, b_s, ox_s, wx_s, rc_s, ry_s, rn_s, rf_s, fa_s, og_s, one_s,
    fa_r, na_r, ya_r, ca_r, cb_r, og_r, x_r, ox_r, wx_r, rc_r, ry_r, rn_r, rf_r, cx_r, cg_r,
):
    r = lax.axis_index("dp")
    t = lax.axis_index("tensor")
    z, s = t // 4, t % 4
    yl, c = s // 2, s % 2
    q, g = z % 4, z // 4
    sib = 2 * yl + (1 - c)
    par = 2 * (1 - yl) + c
    oth = 2 * (1 - yl) + (1 - c)

    def at(gp, qp):
        return (r, (4 * gp + qp) * 4 + s)

    def at_z(zz):
        return (r, zz * 4 + s)

    near = [(q + d) % 4 for d in range(4)]
    core_dev, y_dev = (r, z * 4 + sib), (r, z * 4 + par)

    loads = [
        pltpu.make_async_copy(og, oga.at[r], in_s.at[0]),
        pltpu.make_async_copy(w, wv, in_s.at[1]),
        pltpu.make_async_copy(ctx, own_ctx, in_s.at[2]),
    ]
    for load in loads:
        load.start()

    def greet(semaphore, device):
        pl.semaphore_signal(semaphore, inc=1, device_id=device, device_id_type=MESH)

    rank = jnp.where(g < 4, g, 11 - g)

    def above(gp):
        return (gp if gp < 4 else 11 - gp) > rank

    def below(gp):
        return (gp if gp < 4 else 11 - gp) < rank

    def beside(gp):
        return ((gp - g + 8) % 8 == 1) | ((gp - g + 8) % 8 == 7)

    def straight(b, gp):
        return ((b >= 4) & (gp < 3)) | ((b == 3) & (gp == 0))

    def meets(gp):
        return beside(gp) | straight(g, gp) | straight(gp, g)

    def number(condition):
        return jnp.where(condition, 1, 0)

    ends = (z == 0) | (z == 3) | (z == 28) | (z == 31)
    facing = jnp.where((z == 0) | (z == 28), z + 3, jnp.where(ends, z - 3, z))
    expected = number(ends)
    barrier = pltpu.get_barrier_semaphore()
    for d in (1, -1, 2, -2):

        @pl.when((z + d >= 0) & (z + d < 32))
        def _():
            greet(barrier, at_z(z + d))

        expected += number((z + d >= 0) & (z + d < 32))

    @pl.when(ends)
    def _():
        greet(barrier, at_z(facing))

    partners = [core_dev, y_dev]
    for k in range(1, R):
        partners += [((r + k) % R, z * 4 + sp) for sp in ((s, par, oth) if k % 2 else (s, sib))]
    for gp in range(G):

        @pl.when(above(gp) & meets(gp))
        def _():
            greet(barrier, at(gp, q))

        expected += number(below(gp) & meets(gp))
    for device in partners:
        greet(barrier, device)

    loads[0].wait()
    grad = dot_nt(eye(TOK), oga[r]).astype(BF16)
    loads[1].wait()
    for j in range(16):
        part = jnp.dot(grad, wv[:, j * 384 : (j + 1) * 384], preferred_element_type=F32)
        part = part.T.reshape(2, 2, 2, FB, TOK)
        for i in range(2):
            zz = 2 * j + i
            pf[zz % 4, zz // 4] = part[i]
    order = (2, 1, 3, 0)

    @pl.when(c == 0)
    def _():
        for d in order:
            pc[near[d]] = pf[near[d]].astype(BF16)

    loads[2].wait()
    pl.semaphore_wait(barrier, len(partners) + expected)

    def copy_of(src, dst, ssem, rsem, device):
        return pltpu.make_async_remote_copy(
            src_ref=src, dst_ref=dst, send_sem=ssem, recv_sem=rsem, device_id=device, device_id_type=MESH
        )

    def send(src, dst, ssem, rsem, device):
        copy_of(src, dst, ssem, rsem, device).start()

    def arrived(dst, rsem):
        copy_of(dst, dst, rsem, rsem, core_dev).wait_recv()

    def sent(all_of_it, ssem):
        copy_of(all_of_it, all_of_it, ssem, ssem, core_dev).wait_send()

    def share_grads():
        for k in range(1, R):
            send(oga.at[r], oga.at[r], og_s, og_r, ((r + k) % R, t))

    def half(h):
        return pl.ds(4 * h, 4)

    def hop(k, step, act):
        b, target = (g - step * k + 8) % 8, (g + step + 8) % 8
        block = xt.at[b, q, yl]

        goes = jnp.logical_not(straight(b, target))
        if k == 3:
            goes = (b < 2) if step == 1 else ((b == 2) | (b == 3) | (b == 7))

        @pl.when(goes)
        def _():
            act(copy_of(block, block, fa_s.at[k if step == 1 else 4 + k], fa_r.at[b], at(target, q)))

    def jump(gp, act):
        block = xt.at[g, q, yl]

        @pl.when(straight(g, gp))
        def _():
            act(copy_of(block, block, fa_s.at[8 + gp], fa_r.at[g], at(gp, q)))

    def start(copy):
        copy.start()

    def wait_sent(copy):
        copy.wait_send()

    def rounds(wanted):
        for k, step in ((1, 1), (1, -1), (2, 1), (2, -1), (3, 1), (3, -1), (4, 1)):
            b = (g - step * k + 8) % 8

            @pl.when(wanted(b))
            def _():
                arrived(xt.at[b, q, yl], fa_r.at[b])
                if k < 4:
                    hop(k, step, start)

    held = ((0, 3), (1, 2))

    def spread(d, h):
        mine = xt.at[half(h), near[d], yl]
        send(mine, mine, a_s, ya_r.at[d, h], y_dev)

    def near_sends(h, act):
        own = xt.at[half(h), q, yl]
        way = 2 if h == 0 else -2
        for i, slot, when, target in (
            (0, 2, (z + way >= 0) & (z + way < 32), z + way),
            (1, 0, z < 31, z + 1),
            (2, 1, z > 0, z - 1),
            (3, 0, z == 3, z - 3),
            (4, 1, z == 28, z + 3),
            (5, 2, (z == 2) | (z == 3) if h == 0 else (z == 28) | (z == 29), z - way),
        ):

            @pl.when(when)
            def _():
                act(copy_of(own, own, ns_s.at[i, h], na_r.at[slot, h], at_z(target)))

    def far_done(h):
        near_sends(h, start)
        spread(0, h)

    def near_arrived(h):
        for d, slot in ((3, 0), (1, 1), (2, 2)):
            arrived(xt.at[half(h), near[d], yl], na_r.at[slot, h])
            spread(d, h)
        mine = xt.at[half(h), :, yl]
        send(mine, mine, b_s, ca_r.at[h], core_dev)

    def pair_arrived(d, h):
        arrived(xt.at[half(h), near[d], 1 - yl], ya_r.at[d, h])
        for rr in range(4 * h, 4 * h + 4):

            @pl.when(rr != r)
            def _():
                ours, others = (s, par) if d in held[0] else (sib, oth)
                target = (rr, z * 4 + jnp.where((rr - r + 8) % 2 == 0, ours, others))
                place = held[0].index(d) if d in held[0] else held[1].index(d)
                send(xt.at[rr, near[d]], x2.at[r, near[d]], x_s, x_r.at[r, place], target)

    def pair_done(h):
        for d in (3, 1, 2):
            pair_arrived(d, h)
        theirs = xt.at[half(h), :, 1 - yl]
        send(theirs, theirs, b_s, cb_r.at[h], core_dev)

    def project():
        total = jnp.zeros((ROWS, TOK), F32)
        for j in range(G):
            total += jnp.dot(
                wv[:, j * 768 : (j + 1) * 768], xt[j].reshape(768, TOK), preferred_element_type=F32
            )
        proj[...] = total.astype(BF16)
        x2[r] = xt[r]

    def swap_grads():
        arrived(oga.at[0:7], og_r)
        send(oga, ogx, ox_s, ox_r, core_dev)

    def products(mine):
        arrived(ogx, ox_r)
        rows = jnp.concatenate(
            [jnp.concatenate([grads[k] for k in range(R)], axis=1) for grads in (ogx, oga)], axis=0
        )
        for i, d in enumerate(mine):
            p = near[d]
            for k in range(1, R):
                rr = (r + k) % R
                arrived(x2.at[rr, p], x_r.at[rr, i])
            columns = jnp.concatenate([x2[k, p].reshape(S * FB, TOK) for k in range(R)], axis=1)
            both = dot_nt(rows, columns)
            wgx[i] = both[:ROWS]
            send(wgx.at[i], wgp.at[p], wx_s, wx_r, core_dev)
            wgp[p] = both[ROWS:]

    def collect():
        arrived(wgp.at[0:2], wx_r)
        for p in range(Q):
            wg[:, p * S * FB : (p + 1) * S * FB] = wgp[p]

    @pl.when(c == 0)
    def _():
        xt[g, q, yl, 0] = own_ctx[...]

    def answer():
        for gp in range(G):

            @pl.when(below(gp) & beside(gp))
            def _():
                greet(ok.at[g], at(gp, q))

    def admitted(step):
        for gp in range(G):

            @pl.when(above(gp) & ((gp - g + 8) % 8 == step % 8))
            def _():
                pl.semaphore_wait(ok.at[gp], 1)

    @pl.when(c == 0)
    def _():
        answer()
        for i, d in enumerate(order):
            send(pc.at[near[d]], rc.at[near[d]], rc_s, rc_r.at[i], core_dev)
        arrived(xt.at[g, q, yl, 1], cx_r)
        for gp in range(3):
            jump(gp, start)

        def first_hop(step):
            admitted(step)
            hop(0, step, start)

        @pl.when(g == 0)
        def _():
            first_hop(1)

        first_hop(-1)

        @pl.when(g > 0)
        def _():
            first_hop(1)

        share_grads()

        @pl.when(g < 4)
        def _():
            rounds(lambda b: b < 4)
            far_done(0)
            rounds(lambda b: b >= 4)
            far_done(1)

        @pl.when(g >= 4)
        def _():
            rounds(lambda b: b != (g + 4) % 8)
            far_done(1)
            rounds(lambda b: b == (g + 4) % 8)
            far_done(0)

        pair_arrived(0, 0)
        near_arrived(0)
        pair_arrived(0, 1)
        near_arrived(1)
        pair_done(0)
        pair_done(1)
        swap_grads()
        for k in range(4):
            hop(k, 1, wait_sent)
            hop(k, -1, wait_sent)
        for gp in range(3):
            jump(gp, wait_sent)
        for h in range(2):
            near_sends(h, wait_sent)
        sent(pc, rc_s)
        sent(oga.at[0:7], og_s)
        project()
        sent(x2.at[0:4], a_s)
        sent(x2, b_s)
        sent(oga, ox_s)
        products(held[0])
        arrived(cg_half, cg_r)
        cg[...] = cg_half[...]
        collect()
        sent(x2.at[0:7], x_s)
        sent(wgx, wx_s)

    legs = ((1, 1), (1, -1), (2, 1), (2, -1), (3, 1), (3, -1), (4, 1))

    def leg(k, step):
        last = 4 if step == 1 else 3
        target = (g + step * (last + 1 - k) + 8) % 8
        whole = (target > 3) | ((target == 3) & (step == -1))
        goes = whole | (g < 4)
        fed = whole | ((g - step >= 0) & (g - step < 4))
        return (k - 1 if step == 1 else 3 + k), target, goes, fed

    def rs_copy(slot, there, device):
        return copy_of(fsend.at[slot], frecv.at[there], rf_s.at[slot], rf_r.at[there], device)

    def owner_sum():
        for slot, here in [(6, g >= 0), (3, g != 0)] + [(b + 3, g < 3) for b in range(4, 8)]:

            @pl.when(here)
            def _():
                arrived(frecv.at[slot], rf_r.at[slot])
                pf[q, g, yl] += frecv[slot].astype(F32)

        total = pf[q, g, yl].astype(BF16)
        sent(own_ctx, one_s.at[0])
        cg_half[...] = total[0]
        send(cg_half, cg_half, one_s.at[1], cg_r, core_dev)
        cg[...] = total[1]

    @pl.when(c == 1)
    def _():
        send(own_ctx, xt.at[g, q, yl, 1], one_s.at[0], cx_r, core_dev)
        answer()
        share_grads()
        for i, d in enumerate(order):
            cls = near[d]
            arrived(rc.at[cls], rc_r.at[i])
            ysend[cls] = (pf[cls, :, 1 - yl] + rc[cls, :, 1 - yl].astype(F32)).astype(BF16)
            send(ysend.at[cls], yrecv.at[cls], ry_s, ry_r.at[i], y_dev)
        for i, d in enumerate(order):
            cls = near[d]
            arrived(yrecv.at[cls], ry_r.at[i])
            total = pf[cls, :, yl] + rc[cls, :, yl].astype(F32) + yrecv[cls].astype(F32)
            if d == 0:
                pf[cls, :, yl] = total
            else:
                nsend[d - 1] = total.astype(BF16)
                if d == 2:
                    i0, i1 = jnp.where(z < 2, 4, 2), jnp.where(z > 29, 4, 2)
                    send(nsend.at[1, 0:4], nrecv.at[i0, 0:4], rn_s, rn_r.at[i0], at_z(jnp.where(z < 2, z + 2, z - 2)))
                    i2 = jnp.where(z > 29, 4, 5)
                    send(nsend.at[1, 4:8], nrecv.at[i1, 4:8], rn_s, rn_r.at[i2], at_z(jnp.where(z > 29, z - 2, z + 2)))
                elif d == 1:
                    i0 = jnp.where(z == 31, 3, 1)
                    send(nsend.at[0], nrecv.at[i0], rn_s, rn_r.at[i0], at_z(jnp.where(z == 31, z - 3, z + 1)))
                else:
                    i0 = jnp.where(z == 0, 3, 0)
                    send(nsend.at[2], nrecv.at[i0], rn_s, rn_r.at[i0], at_z(jnp.where(z == 0, z + 3, z - 1)))
        for here, ref, sem in (
            (z < 31, nrecv.at[0], 0),
            (z > 0, nrecv.at[1], 1),
            (z < 30, nrecv.at[2, 0:4], 2),
            (z > 1, nrecv.at[2, 4:8], 5),
        ):

            @pl.when(here)
            def _():
                arrived(ref, rn_r.at[sem])

            @pl.when(jnp.logical_not(here))
            def _():
                ref[...] = jnp.zeros(ref.shape, BF16)

        window = pf[q, :, yl] + nrecv[0].astype(F32) + nrecv[1].astype(F32) + nrecv[2].astype(F32)
        pf[q, :, yl] = window
        for here, ref, sem, low, high in (
            ((z == 3) | (z == 28), nrecv.at[3], 3, 0, 8),
            ((z == 2) | (z == 3), nrecv.at[4, 0:4], 4, 0, 4),
            ((z == 28) | (z == 29), nrecv.at[4, 4:8], 4, 4, 8),
        ):

            @pl.when(here)
            def _():
                arrived(ref, rn_r.at[sem])
                pf[q, low:high, yl] += ref[...].astype(F32)

        admitted(1)
        admitted(-1)
        for gp in range(3):

            @pl.when(g >= 4)
            def _():
                fsend[7 + gp] = pf[q, gp, yl].astype(BF16)
                rs_copy(7 + gp, 3 + g, at(gp, q)).start()

        def pass_on(k, step, early):
            slot, target, goes, fed = leg(k, step)
            goes = goes & early(target)

            @pl.when(goes)
            def _():
                fsend[slot] = pf[q, target, yl].astype(BF16)

            if (k, step) == (1, -1):

                @pl.when(goes & (g == 6))
                def _():
                    arrived(frecv.at[11], rf_r.at[11])
                    fsend[slot] = (pf[q, target, yl] + frecv[11].astype(F32)).astype(BF16)

            if k > 1:

                @pl.when(goes & fed)
                def _():
                    arrived(frecv.at[slot - 1], rf_r.at[slot - 1])
                    fsend[slot] = (pf[q, target, yl] + frecv[slot - 1].astype(F32)).astype(BF16)

            @pl.when(goes)
            def _():
                rs_copy(slot, slot, at((g + step + 8) % 8, q)).start()

        for k, step in legs[:2]:
            pass_on(k, step, lambda target: target != 3)

        @pl.when(g == 7)
        def _():
            fsend[10] = pf[q, 3, yl].astype(BF16)
            rs_copy(10, 11, at(6, q)).start()

        for k, step in legs[2:]:
            pass_on(k, step, lambda target: target != 3)
        for k, step in legs:
            pass_on(k, step, lambda target: target == 3)

        swap_grads()
        sent(ysend, ry_s)
        sent(nsend, rn_s)
        sent(oga.at[0:7], og_s)
        for h in range(2):
            arrived(xt.at[half(h), :, yl], ca_r.at[h])
            arrived(xt.at[half(h), :, 1 - yl], cb_r.at[h])
        project()
        for gp in range(3):

            @pl.when(g >= 4)
            def _():
                rs_copy(7 + gp, 3 + g, at(gp, q)).wait_send()

        for k, step in legs:
            slot, target, goes, fed = leg(k, step)

            @pl.when(goes)
            def _():
                rs_copy(slot, slot, at((g + step + 8) % 8, q)).wait_send()

        @pl.when(g == 7)
        def _():
            rs_copy(10, 11, at(6, q)).wait_send()

        @pl.when(g >= 4)
        def _():
            owner_sum()

        products(held[1])

        @pl.when(g < 4)
        def _():
            owner_sum()

        collect()
        sent(cg_half, one_s.at[1])
        sent(oga, ox_s)
        sent(wgx, wx_s)


def local(context, w_out, out_grad):
    vmem = pl.BlockSpec(memory_space=pltpu.VMEM)
    dma = pltpu.SemaphoreType.DMA
    projected, context_grad, weight_grad = pl.pallas_call(
        kernel,
        out_shape=(
            jax.ShapeDtypeStruct((ROWS, TOK), BF16),
            jax.ShapeDtypeStruct((FB, TOK), BF16),
            jax.ShapeDtypeStruct((ROWS, Q * S * FB), F32),
        ),
        in_specs=[pl.BlockSpec(memory_space=pltpu.HBM)] * 3,
        out_specs=(vmem,) * 3,
        scratch_shapes=[
            pltpu.VMEM((G, Q, 2, 2, FB, TOK), BF16),
            pltpu.VMEM((ROWS, G * Q * S * FB), BF16),
            pltpu.VMEM((Q, G, 2, 2, FB, TOK), F32),
            pltpu.VMEM((Q, G, 2, 2, FB, TOK), BF16),
            pltpu.VMEM((Q, G, 2, 2, FB, TOK), BF16),
            pltpu.VMEM((Q, G, 2, FB, TOK), BF16),
            pltpu.VMEM((Q, G, 2, FB, TOK), BF16),
            pltpu.VMEM((3, G, 2, FB, TOK), BF16),
            pltpu.VMEM((5, G, 2, FB, TOK), BF16),
            pltpu.VMEM((11, 2, FB, TOK), BF16),
            pltpu.VMEM((12, 2, FB, TOK), BF16),
            pltpu.VMEM((R, ROWS, TOK), BF16),
            pltpu.VMEM((R, Q, 2, 2, FB, TOK), BF16),
            pltpu.VMEM((FB, TOK), BF16),
            pltpu.VMEM((FB, TOK), BF16),
            pltpu.VMEM((R, ROWS, TOK), BF16),
            pltpu.VMEM((Q, ROWS, S * FB), F32),
            pltpu.VMEM((2, ROWS, S * FB), F32),
            pltpu.SemaphoreType.REGULAR((G,)), dma((3,)),
            dma, dma((6, 2)), dma, dma, dma, dma, dma, dma, dma, dma((11,)), dma((11,)), dma, dma((2,)),
            dma((G,)), dma((3, 2)), dma((Q, 2)), dma((2,)), dma((2,)), dma, dma((R, 2)), dma, dma, dma((Q,)), dma((Q,)),
            dma((6,)), dma((12,)), dma, dma,
        ],
        compiler_params=pltpu.CompilerParams(
            collective_id=0, has_side_effects=True, vmem_limit_bytes=52 * 2**20
        ),
        cost_estimate=pl.CostEstimate(
            flops=6 * TOK * ROWS * 6144, bytes_accessed=4_000_000, transcendentals=0
        ),
    )(context.T, w_out, out_grad.T)
    return projected.T, context_grad.T, weight_grad


def solution(mesh):
    placed = (P("dp", "tensor"), P("tensor", None), P("dp", "tensor"))
    return jax.shard_map(
        local,
        mesh=mesh,
        in_specs=placed,
        out_specs=(P("dp", "tensor"), P("dp", "tensor"), P("tensor", "dp")),
        check_vma=False,
    )
```

```python
import jax
import jax.numpy as jnp
from jax import lax
from jax.experimental import pallas as pl
from jax.experimental.pallas import tpu as pltpu
from jax.sharding import PartitionSpec as P

MESH = pl.DeviceIdType.MESH
F32, BF16 = jnp.float32, jnp.bfloat16
R, G, Q, S, FB, TOK, ROWS = 8, 8, 4, 4, 48, 128, 144


def dot_nt(a, b):
    return lax.dot_general(a, b, (((1,), (1,)), ((), ())), preferred_element_type=F32)


def eye(n):
    return (
        lax.broadcasted_iota(jnp.int32, (n, n), 0) == lax.broadcasted_iota(jnp.int32, (n, n), 1)
    ).astype(F32).astype(BF16)


def kernel(
    both, w, proj, cg, wg,
    xt, wv, pf, pc, rc, ysend, yrecv, nsend, nrecv, fsend, frecv, oga, x2, own_ctx, cg_half, ogx, wgp, wgx,
    ok, in_s, a_s, ns_s, x_s, b_s, ox_s, wx_s, rc_s, ry_s, rn_s, rf_s, fa_s, og_s, one_s,
    fa_r, na_r, ya_r, ca_r, cb_r, og_r, x_r, ox_r, wx_r, rc_r, ry_r, rn_r, rf_r, cx_r, cg_r,
):
    r = lax.axis_index("dp")
    t = lax.axis_index("tensor")
    z, s = t // 4, t % 4
    yl, c = s // 2, s % 2
    q, g = z % 4, z // 4
    sib = 2 * yl + (1 - c)
    par = 2 * (1 - yl) + c
    oth = 2 * (1 - yl) + (1 - c)

    def at(gp, qp):
        return (r, (4 * gp + qp) * 4 + s)

    def at_z(zz):
        return (r, zz * 4 + s)

    near = [(q + d) % 4 for d in range(4)]
    core_dev, y_dev = (r, z * 4 + sib), (r, z * 4 + par)

    loads = [
        pltpu.make_async_copy(both.at[0:ROWS], oga.at[r], in_s.at[0]),
        pltpu.make_async_copy(w, wv, in_s.at[1]),
        pltpu.make_async_copy(both.at[ROWS : ROWS + FB], own_ctx, in_s.at[2]),
    ]
    for load in loads:
        load.start()

    def greet(semaphore, device):
        pl.semaphore_signal(semaphore, inc=1, device_id=device, device_id_type=MESH)

    rank = jnp.where(g < 4, g, 11 - g)

    def above(gp):
        return (gp if gp < 4 else 11 - gp) > rank

    def below(gp):
        return (gp if gp < 4 else 11 - gp) < rank

    def beside(gp):
        return ((gp - g + 8) % 8 == 1) | ((gp - g + 8) % 8 == 7)

    def straight(b, gp):
        return ((b >= 4) & (gp < 3)) | ((b == 3) & (gp == 0))

    def meets(gp):
        return beside(gp) | straight(g, gp) | straight(gp, g)

    def number(condition):
        return jnp.where(condition, 1, 0)

    ends = (z == 0) | (z == 3) | (z == 28) | (z == 31)
    facing = jnp.where((z == 0) | (z == 28), z + 3, jnp.where(ends, z - 3, z))
    expected = number(ends)
    barrier = pltpu.get_barrier_semaphore()
    for d in (1, -1, 2, -2):

        @pl.when((z + d >= 0) & (z + d < 32))
        def _():
            greet(barrier, at_z(z + d))

        expected += number((z + d >= 0) & (z + d < 32))

    @pl.when(ends)
    def _():
        greet(barrier, at_z(facing))

    partners = [core_dev, y_dev]
    for k in range(1, R):
        partners += [((r + k) % R, z * 4 + sp) for sp in ((s, par, oth) if k % 2 else (s, sib))]
    for gp in range(G):

        @pl.when(above(gp) & meets(gp))
        def _():
            greet(barrier, at(gp, q))

        expected += number(below(gp) & meets(gp))
    for device in partners:
        greet(barrier, device)

    loads[0].wait()
    grad = dot_nt(eye(TOK), oga[r]).astype(BF16)
    loads[1].wait()
    for j in range(16):
        part = jnp.dot(grad, wv[:, j * 384 : (j + 1) * 384], preferred_element_type=F32)
        part = part.T.reshape(2, 2, 2, FB, TOK)
        for i in range(2):
            zz = 2 * j + i
            pf[zz % 4, zz // 4] = part[i]
    order = (2, 1, 3, 0)

    @pl.when(c == 0)
    def _():
        for d in order:
            pc[near[d]] = pf[near[d]].astype(BF16)

    loads[2].wait()
    pl.semaphore_wait(barrier, len(partners) + expected)

    def copy_of(src, dst, ssem, rsem, device):
        return pltpu.make_async_remote_copy(
            src_ref=src, dst_ref=dst, send_sem=ssem, recv_sem=rsem, device_id=device, device_id_type=MESH
        )

    def send(src, dst, ssem, rsem, device):
        copy_of(src, dst, ssem, rsem, device).start()

    def arrived(dst, rsem):
        copy_of(dst, dst, rsem, rsem, core_dev).wait_recv()

    def sent(all_of_it, ssem):
        copy_of(all_of_it, all_of_it, ssem, ssem, core_dev).wait_send()

    def share_grads():
        for k in range(1, R):
            send(oga.at[r], oga.at[r], og_s, og_r, ((r + k) % R, t))

    def half(h):
        return pl.ds(4 * h, 4)

    def hop(k, step, act):
        b, target = (g - step * k + 8) % 8, (g + step + 8) % 8
        block = xt.at[b, q, yl]

        goes = jnp.logical_not(straight(b, target))
        if k == 3:
            goes = (b < 2) if step == 1 else ((b == 2) | (b == 3) | (b == 7))

        @pl.when(goes)
        def _():
            act(copy_of(block, block, fa_s.at[k if step == 1 else 4 + k], fa_r.at[b], at(target, q)))

    def jump(gp, act):
        block = xt.at[g, q, yl]

        @pl.when(straight(g, gp))
        def _():
            act(copy_of(block, block, fa_s.at[8 + gp], fa_r.at[g], at(gp, q)))

    def start(copy):
        copy.start()

    def wait_sent(copy):
        copy.wait_send()

    def rounds(wanted):
        for k, step in ((1, 1), (1, -1), (2, 1), (2, -1), (3, 1), (3, -1), (4, 1)):
            b = (g - step * k + 8) % 8

            @pl.when(wanted(b))
            def _():
                arrived(xt.at[b, q, yl], fa_r.at[b])
                if k < 4:
                    hop(k, step, start)

    held = ((0, 3), (1, 2))

    def spread(d, h):
        mine = xt.at[half(h), near[d], yl]
        send(mine, mine, a_s, ya_r.at[d, h], y_dev)

    def near_sends(h, act):
        own = xt.at[half(h), q, yl]
        way = 2 if h == 0 else -2
        for i, slot, when, target in (
            (0, 2, (z + way >= 0) & (z + way < 32), z + way),
            (1, 0, z < 31, z + 1),
            (2, 1, z > 0, z - 1),
            (3, 0, z == 3, z - 3),
            (4, 1, z == 28, z + 3),
            (5, 2, (z == 2) | (z == 3) if h == 0 else (z == 28) | (z == 29), z - way),
        ):

            @pl.when(when)
            def _():
                act(copy_of(own, own, ns_s.at[i, h], na_r.at[slot, h], at_z(target)))

    def far_done(h):
        near_sends(h, start)
        spread(0, h)

    def near_arrived(h):
        for d, slot in ((3, 0), (1, 1), (2, 2)):
            arrived(xt.at[half(h), near[d], yl], na_r.at[slot, h])
            spread(d, h)
        mine = xt.at[half(h), :, yl]
        send(mine, mine, b_s, ca_r.at[h], core_dev)

    def pair_arrived(d, h):
        arrived(xt.at[half(h), near[d], 1 - yl], ya_r.at[d, h])
        for rr in range(4 * h, 4 * h + 4):

            @pl.when(rr != r)
            def _():
                ours, others = (s, par) if d in held[0] else (sib, oth)
                target = (rr, z * 4 + jnp.where((rr - r + 8) % 2 == 0, ours, others))
                place = held[0].index(d) if d in held[0] else held[1].index(d)
                send(xt.at[rr, near[d]], x2.at[r, near[d]], x_s, x_r.at[r, place], target)

    def pair_done(h):
        for d in (3, 1, 2):
            pair_arrived(d, h)
        theirs = xt.at[half(h), :, 1 - yl]
        send(theirs, theirs, b_s, cb_r.at[h], core_dev)

    def project():
        total = jnp.zeros((ROWS, TOK), F32)
        for j in range(G):
            total += jnp.dot(
                wv[:, j * 768 : (j + 1) * 768], xt[j].reshape(768, TOK), preferred_element_type=F32
            )
        proj[...] = total.astype(BF16)
        x2[r] = xt[r]

    def swap_grads():
        arrived(oga.at[0:7], og_r)
        send(oga, ogx, ox_s, ox_r, core_dev)

    def products(mine):
        arrived(ogx, ox_r)
        rows = jnp.concatenate(
            [jnp.concatenate([grads[k] for k in range(R)], axis=1) for grads in (ogx, oga)], axis=0
        )
        for i, d in enumerate(mine):
            p = near[d]
            for k in range(1, R):
                rr = (r + k) % R
                arrived(x2.at[rr, p], x_r.at[rr, i])
            columns = jnp.concatenate([x2[k, p].reshape(S * FB, TOK) for k in range(R)], axis=1)
            both = dot_nt(rows, columns)
            wgx[i] = both[:ROWS]
            send(wgx.at[i], wgp.at[p], wx_s, wx_r, core_dev)
            wgp[p] = both[ROWS:]

    def collect():
        arrived(wgp.at[0:2], wx_r)
        for p in range(Q):
            wg[:, p * S * FB : (p + 1) * S * FB] = wgp[p]

    @pl.when(c == 0)
    def _():
        xt[g, q, yl, 0] = own_ctx[...]

    def answer():
        for gp in range(G):

            @pl.when(below(gp) & beside(gp))
            def _():
                greet(ok.at[g], at(gp, q))

    def admitted(step):
        for gp in range(G):

            @pl.when(above(gp) & ((gp - g + 8) % 8 == step % 8))
            def _():
                pl.semaphore_wait(ok.at[gp], 1)

    @pl.when(c == 0)
    def _():
        answer()
        for i, d in enumerate(order):
            send(pc.at[near[d]], rc.at[near[d]], rc_s, rc_r.at[i], core_dev)
        arrived(xt.at[g, q, yl, 1], cx_r)
        for gp in range(3):
            jump(gp, start)

        def first_hop(step):
            admitted(step)
            hop(0, step, start)

        @pl.when(g == 0)
        def _():
            first_hop(1)

        first_hop(-1)

        @pl.when(g > 0)
        def _():
            first_hop(1)

        share_grads()

        @pl.when(g < 4)
        def _():
            rounds(lambda b: b < 4)
            far_done(0)
            rounds(lambda b: b >= 4)
            far_done(1)

        @pl.when(g >= 4)
        def _():
            rounds(lambda b: b != (g + 4) % 8)
            far_done(1)
            rounds(lambda b: b == (g + 4) % 8)
            far_done(0)

        pair_arrived(0, 0)
        near_arrived(0)
        pair_arrived(0, 1)
        near_arrived(1)
        pair_done(0)
        pair_done(1)
        swap_grads()
        for k in range(4):
            hop(k, 1, wait_sent)
            hop(k, -1, wait_sent)
        for gp in range(3):
            jump(gp, wait_sent)
        for h in range(2):
            near_sends(h, wait_sent)
        sent(pc, rc_s)
        sent(oga.at[0:7], og_s)
        project()
        sent(x2.at[0:4], a_s)
        sent(x2, b_s)
        sent(oga, ox_s)
        products(held[0])
        arrived(cg_half, cg_r)
        cg[...] = cg_half[...]
        collect()
        sent(x2.at[0:7], x_s)
        sent(wgx, wx_s)

    legs = ((1, 1), (1, -1), (2, 1), (2, -1), (3, 1), (3, -1), (4, 1))

    def leg(k, step):
        last = 4 if step == 1 else 3
        target = (g + step * (last + 1 - k) + 8) % 8
        whole = (target > 3) | ((target == 3) & (step == -1))
        goes = whole | (g < 4)
        fed = whole | ((g - step >= 0) & (g - step < 4))
        return (k - 1 if step == 1 else 3 + k), target, goes, fed

    def rs_copy(slot, there, device):
        return copy_of(fsend.at[slot], frecv.at[there], rf_s.at[slot], rf_r.at[there], device)

    def owner_sum():
        for slot, here in [(6, g >= 0), (3, g != 0)] + [(b + 3, g < 3) for b in range(4, 8)]:

            @pl.when(here)
            def _():
                arrived(frecv.at[slot], rf_r.at[slot])
                pf[q, g, yl] += frecv[slot].astype(F32)

        total = pf[q, g, yl].astype(BF16)
        sent(own_ctx, one_s.at[0])
        cg_half[...] = total[0]
        send(cg_half, cg_half, one_s.at[1], cg_r, core_dev)
        cg[...] = total[1]

    @pl.when(c == 1)
    def _():
        send(own_ctx, xt.at[g, q, yl, 1], one_s.at[0], cx_r, core_dev)
        answer()
        share_grads()
        for i, d in enumerate(order):
            cls = near[d]
            arrived(rc.at[cls], rc_r.at[i])
            ysend[cls] = (pf[cls, :, 1 - yl] + rc[cls, :, 1 - yl].astype(F32)).astype(BF16)
            send(ysend.at[cls], yrecv.at[cls], ry_s, ry_r.at[i], y_dev)
        for i, d in enumerate(order):
            cls = near[d]
            arrived(yrecv.at[cls], ry_r.at[i])
            total = pf[cls, :, yl] + rc[cls, :, yl].astype(F32) + yrecv[cls].astype(F32)
            if d == 0:
                pf[cls, :, yl] = total
            else:
                nsend[d - 1] = total.astype(BF16)
                if d == 2:
                    i0, i1 = jnp.where(z < 2, 4, 2), jnp.where(z > 29, 4, 2)
                    send(nsend.at[1, 0:4], nrecv.at[i0, 0:4], rn_s, rn_r.at[i0], at_z(jnp.where(z < 2, z + 2, z - 2)))
                    i2 = jnp.where(z > 29, 4, 5)
                    send(nsend.at[1, 4:8], nrecv.at[i1, 4:8], rn_s, rn_r.at[i2], at_z(jnp.where(z > 29, z - 2, z + 2)))
                elif d == 1:
                    i0 = jnp.where(z == 31, 3, 1)
                    send(nsend.at[0], nrecv.at[i0], rn_s, rn_r.at[i0], at_z(jnp.where(z == 31, z - 3, z + 1)))
                else:
                    i0 = jnp.where(z == 0, 3, 0)
                    send(nsend.at[2], nrecv.at[i0], rn_s, rn_r.at[i0], at_z(jnp.where(z == 0, z + 3, z - 1)))
        for here, ref, sem in (
            (z < 31, nrecv.at[0], 0),
            (z > 0, nrecv.at[1], 1),
            (z < 30, nrecv.at[2, 0:4], 2),
            (z > 1, nrecv.at[2, 4:8], 5),
        ):

            @pl.when(here)
            def _():
                arrived(ref, rn_r.at[sem])

            @pl.when(jnp.logical_not(here))
            def _():
                ref[...] = jnp.zeros(ref.shape, BF16)

        window = pf[q, :, yl] + nrecv[0].astype(F32) + nrecv[1].astype(F32) + nrecv[2].astype(F32)
        pf[q, :, yl] = window
        for here, ref, sem, low, high in (
            ((z == 3) | (z == 28), nrecv.at[3], 3, 0, 8),
            ((z == 2) | (z == 3), nrecv.at[4, 0:4], 4, 0, 4),
            ((z == 28) | (z == 29), nrecv.at[4, 4:8], 4, 4, 8),
        ):

            @pl.when(here)
            def _():
                arrived(ref, rn_r.at[sem])
                pf[q, low:high, yl] += ref[...].astype(F32)

        admitted(1)
        admitted(-1)
        for gp in range(3):

            @pl.when(g >= 4)
            def _():
                fsend[7 + gp] = pf[q, gp, yl].astype(BF16)
                rs_copy(7 + gp, 3 + g, at(gp, q)).start()

        def pass_on(k, step, early):
            slot, target, goes, fed = leg(k, step)
            goes = goes & early(target)

            @pl.when(goes)
            def _():
                fsend[slot] = pf[q, target, yl].astype(BF16)

            if (k, step) == (1, -1):

                @pl.when(goes & (g == 6))
                def _():
                    arrived(frecv.at[11], rf_r.at[11])
                    fsend[slot] = (pf[q, target, yl] + frecv[11].astype(F32)).astype(BF16)

            if k > 1:

                @pl.when(goes & fed)
                def _():
                    arrived(frecv.at[slot - 1], rf_r.at[slot - 1])
                    fsend[slot] = (pf[q, target, yl] + frecv[slot - 1].astype(F32)).astype(BF16)

            @pl.when(goes)
            def _():
                rs_copy(slot, slot, at((g + step + 8) % 8, q)).start()

        for k, step in legs[:2]:
            pass_on(k, step, lambda target: target != 3)

        @pl.when(g == 7)
        def _():
            fsend[10] = pf[q, 3, yl].astype(BF16)
            rs_copy(10, 11, at(6, q)).start()

        for k, step in legs[2:]:
            pass_on(k, step, lambda target: target != 3)
        for k, step in legs:
            pass_on(k, step, lambda target: target == 3)

        swap_grads()
        sent(ysend, ry_s)
        sent(nsend, rn_s)
        sent(oga.at[0:7], og_s)
        for h in range(2):
            arrived(xt.at[half(h), :, yl], ca_r.at[h])
            arrived(xt.at[half(h), :, 1 - yl], cb_r.at[h])
        project()
        for gp in range(3):

            @pl.when(g >= 4)
            def _():
                rs_copy(7 + gp, 3 + g, at(gp, q)).wait_send()

        for k, step in legs:
            slot, target, goes, fed = leg(k, step)

            @pl.when(goes)
            def _():
                rs_copy(slot, slot, at((g + step + 8) % 8, q)).wait_send()

        @pl.when(g == 7)
        def _():
            rs_copy(10, 11, at(6, q)).wait_send()

        @pl.when(g >= 4)
        def _():
            owner_sum()

        products(held[1])

        @pl.when(g < 4)
        def _():
            owner_sum()

        collect()
        sent(cg_half, one_s.at[1])
        sent(oga, ox_s)
        sent(wgx, wx_s)


def local(context, w_out, out_grad):
    vmem = pl.BlockSpec(memory_space=pltpu.VMEM)
    dma = pltpu.SemaphoreType.DMA
    projected, context_grad, weight_grad = pl.pallas_call(
        kernel,
        out_shape=(
            jax.ShapeDtypeStruct((ROWS, TOK), BF16),
            jax.ShapeDtypeStruct((FB, TOK), BF16),
            jax.ShapeDtypeStruct((ROWS, Q * S * FB), F32),
        ),
        in_specs=[pl.BlockSpec(memory_space=pltpu.HBM)] * 2,
        out_specs=(vmem,) * 3,
        scratch_shapes=[
            pltpu.VMEM((G, Q, 2, 2, FB, TOK), BF16),
            pltpu.VMEM((ROWS, G * Q * S * FB), BF16),
            pltpu.VMEM((Q, G, 2, 2, FB, TOK), F32),
            pltpu.VMEM((Q, G, 2, 2, FB, TOK), BF16),
            pltpu.VMEM((Q, G, 2, 2, FB, TOK), BF16),
            pltpu.VMEM((Q, G, 2, FB, TOK), BF16),
            pltpu.VMEM((Q, G, 2, FB, TOK), BF16),
            pltpu.VMEM((3, G, 2, FB, TOK), BF16),
            pltpu.VMEM((5, G, 2, FB, TOK), BF16),
            pltpu.VMEM((11, 2, FB, TOK), BF16),
            pltpu.VMEM((12, 2, FB, TOK), BF16),
            pltpu.VMEM((R, ROWS, TOK), BF16),
            pltpu.VMEM((R, Q, 2, 2, FB, TOK), BF16),
            pltpu.VMEM((FB, TOK), BF16),
            pltpu.VMEM((FB, TOK), BF16),
            pltpu.VMEM((R, ROWS, TOK), BF16),
            pltpu.VMEM((Q, ROWS, S * FB), F32),
            pltpu.VMEM((2, ROWS, S * FB), F32),
            pltpu.SemaphoreType.REGULAR((G,)), dma((3,)),
            dma, dma((6, 2)), dma, dma, dma, dma, dma, dma, dma, dma((11,)), dma((11,)), dma, dma((2,)),
            dma((G,)), dma((3, 2)), dma((Q, 2)), dma((2,)), dma((2,)), dma, dma((R, 2)), dma, dma, dma((Q,)), dma((Q,)),
            dma((6,)), dma((12,)), dma, dma,
        ],
        compiler_params=pltpu.CompilerParams(
            collective_id=0, has_side_effects=True, vmem_limit_bytes=52 * 2**20
        ),
        cost_estimate=pl.CostEstimate(
            flops=6 * TOK * ROWS * 6144, bytes_accessed=4_000_000, transcendentals=0
        ),
    )(jnp.concatenate([out_grad.T, context.T], axis=0), w_out)
    return projected.T, context_grad.T, weight_grad


def solution(mesh):
    placed = (P("dp", "tensor"), P("tensor", None), P("dp", "tensor"))
    return jax.shard_map(
        local,
        mesh=mesh,
        in_specs=placed,
        out_specs=(P("dp", "tensor"), P("dp", "tensor"), P("tensor", "dp")),
        check_vma=False,
    )
```

```python
import jax
import jax.numpy as jnp
from jax import lax
from jax.experimental import pallas as pl
from jax.experimental.pallas import tpu as pltpu
from jax.sharding import PartitionSpec as P

MESH = pl.DeviceIdType.MESH
F32, BF16 = jnp.float32, jnp.bfloat16
R, G, Q, S, FB, TOK, ROWS = 8, 8, 4, 4, 48, 128, 144


def dot_nt(a, b):
    return lax.dot_general(a, b, (((1,), (1,)), ((), ())), preferred_element_type=F32)


def eye(n):
    return (
        lax.broadcasted_iota(jnp.int32, (n, n), 0) == lax.broadcasted_iota(jnp.int32, (n, n), 1)
    ).astype(F32).astype(BF16)


def kernel(
    both, w, proj, cg, wg,
    xt, wv, pf, pc, rc, ysend, yrecv, nsend, nrecv, fsend, frecv, oga, x2, own_ctx, cg_half, ogx, wgp, wgx,
    ok, in_s, a_s, ns_s, x_s, b_s, ox_s, wx_s, rc_s, ry_s, rn_s, rf_s, fa_s, og_s, one_s,
    fa_r, na_r, ya_r, ca_r, cb_r, og_r, x_r, ox_r, wx_r, rc_r, ry_r, rn_r, rf_r, cx_r, cg_r,
):
    r = lax.axis_index("dp")
    t = lax.axis_index("tensor")
    z, s = t // 4, t % 4
    yl, c = s // 2, s % 2
    q, g = z % 4, z // 4
    sib = 2 * yl + (1 - c)
    par = 2 * (1 - yl) + c
    oth = 2 * (1 - yl) + (1 - c)

    def at(gp, qp):
        return (r, (4 * gp + qp) * 4 + s)

    def at_z(zz):
        return (r, zz * 4 + s)

    near = [(q + d) % 4 for d in range(4)]
    core_dev, y_dev = (r, z * 4 + sib), (r, z * 4 + par)

    loads = [
        pltpu.make_async_copy(both.at[0:ROWS], oga.at[r], in_s.at[0]),
        pltpu.make_async_copy(w, wv, in_s.at[1]),
        pltpu.make_async_copy(both.at[ROWS : ROWS + FB], own_ctx, in_s.at[2]),
    ]
    for load in loads:
        load.start()

    def greet(semaphore, device):
        pl.semaphore_signal(semaphore, inc=1, device_id=device, device_id_type=MESH)

    rank = jnp.where(g < 4, g, 11 - g)

    def above(gp):
        return (gp if gp < 4 else 11 - gp) > rank

    def below(gp):
        return (gp if gp < 4 else 11 - gp) < rank

    def beside(gp):
        return ((gp - g + 8) % 8 == 1) | ((gp - g + 8) % 8 == 7)

    def straight(b, gp):
        return ((b >= 4) & (gp < 3)) | ((b == 3) & (gp == 0))

    def meets(gp):
        return beside(gp) | straight(g, gp) | straight(gp, g)

    def number(condition):
        return jnp.where(condition, 1, 0)

    ends = (z == 0) | (z == 3) | (z == 28) | (z == 31)
    facing = jnp.where((z == 0) | (z == 28), z + 3, jnp.where(ends, z - 3, z))
    expected = number(ends)
    barrier = pltpu.get_barrier_semaphore()
    for d in (1, -1, 2, -2):

        @pl.when((z + d >= 0) & (z + d < 32))
        def _():
            greet(barrier, at_z(z + d))

        expected += number((z + d >= 0) & (z + d < 32))

    @pl.when(ends)
    def _():
        greet(barrier, at_z(facing))

    partners = [core_dev, y_dev]
    for k in range(1, R):
        partners += [((r + k) % R, z * 4 + sp) for sp in ((s, par, oth) if k % 2 else (s, sib))]
    for gp in range(G):

        @pl.when(above(gp) & meets(gp))
        def _():
            greet(barrier, at(gp, q))

        expected += number(below(gp) & meets(gp))
    for device in partners:
        greet(barrier, device)

    loads[0].wait()
    grad = dot_nt(eye(TOK), oga[r]).astype(BF16)
    loads[1].wait()
    for j in range(16):
        part = jnp.dot(grad, wv[:, j * 384 : (j + 1) * 384], preferred_element_type=F32)
        part = part.T.reshape(2, 2, 2, FB, TOK)
        for i in range(2):
            zz = 2 * j + i
            pf[zz % 4, zz // 4] = part[i]
    order = (2, 1, 3, 0)

    @pl.when(c == 0)
    def _():
        for d in order:
            pc[near[d]] = pf[near[d]].astype(BF16)

    loads[2].wait()
    pl.semaphore_wait(barrier, len(partners) + expected)

    def copy_of(src, dst, ssem, rsem, device):
        return pltpu.make_async_remote_copy(
            src_ref=src, dst_ref=dst, send_sem=ssem, recv_sem=rsem, device_id=device, device_id_type=MESH
        )

    def send(src, dst, ssem, rsem, device):
        copy_of(src, dst, ssem, rsem, device).start()

    def arrived(dst, rsem):
        copy_of(dst, dst, rsem, rsem, core_dev).wait_recv()

    def sent(all_of_it, ssem):
        copy_of(all_of_it, all_of_it, ssem, ssem, core_dev).wait_send()

    def share_grads():
        for k in range(1, R):
            send(oga.at[r], oga.at[r], og_s, og_r, ((r + k) % R, t))

    def half(h):
        return pl.ds(4 * h, 4)

    def hop(k, step, act):
        b, target = (g - step * k + 8) % 8, (g + step + 8) % 8
        block = xt.at[b, q, yl]

        goes = jnp.logical_not(straight(b, target))
        if k == 3:
            goes = (b < 2) if step == 1 else ((b == 2) | (b == 3) | (b == 7))

        @pl.when(goes)
        def _():
            act(copy_of(block, block, fa_s.at[k if step == 1 else 4 + k], fa_r.at[b], at(target, q)))

    def jump(gp, act):
        block = xt.at[g, q, yl]

        @pl.when(straight(g, gp))
        def _():
            act(copy_of(block, block, fa_s.at[8 + gp], fa_r.at[g], at(gp, q)))

    def start(copy):
        copy.start()

    def wait_sent(copy):
        copy.wait_send()

    def rounds(wanted):
        for k, step in ((1, 1), (1, -1), (2, 1), (2, -1), (3, 1), (3, -1), (4, 1)):
            b = (g - step * k + 8) % 8

            @pl.when(wanted(b))
            def _():
                arrived(xt.at[b, q, yl], fa_r.at[b])
                if k < 4:
                    hop(k, step, start)

    held = ((0, 3), (1, 2))

    def spread(d, h):
        mine = xt.at[half(h), near[d], yl]
        send(mine, mine, a_s, ya_r.at[d, h], y_dev)

    def near_sends(h, act):
        own = xt.at[half(h), q, yl]
        way = 2 if h == 0 else -2
        for i, slot, when, target in (
            (0, 2, (z + way >= 0) & (z + way < 32), z + way),
            (1, 0, z < 31, z + 1),
            (2, 1, z > 0, z - 1),
            (3, 0, z == 3, z - 3),
            (4, 1, z == 28, z + 3),
            (5, 2, (z == 2) | (z == 3) if h == 0 else (z == 28) | (z == 29), z - way),
        ):

            @pl.when(when)
            def _():
                act(copy_of(own, own, ns_s.at[i, h], na_r.at[slot, h], at_z(target)))

    def far_done(h):
        near_sends(h, start)
        spread(0, h)

    def near_arrived(h):
        for d, slot in ((3, 0), (1, 1), (2, 2)):
            arrived(xt.at[half(h), near[d], yl], na_r.at[slot, h])
            spread(d, h)
        mine = xt.at[half(h), :, yl]
        send(mine, mine, b_s, ca_r.at[h], core_dev)

    def pair_arrived(d, h):
        arrived(xt.at[half(h), near[d], 1 - yl], ya_r.at[d, h])
        for k in range(4):
            rr = 4 * h + (r + k + 1) % 4

            @pl.when(rr != r)
            def _():
                ours, others = (s, par) if d in held[0] else (sib, oth)
                target = (rr, z * 4 + jnp.where((rr - r + 8) % 2 == 0, ours, others))
                place = held[0].index(d) if d in held[0] else held[1].index(d)
                send(xt.at[rr, near[d]], x2.at[r, near[d]], x_s, x_r.at[r, place], target)

    def pair_done(h):
        for d in (3, 1, 2):
            pair_arrived(d, h)
        theirs = xt.at[half(h), :, 1 - yl]
        send(theirs, theirs, b_s, cb_r.at[h], core_dev)

    def project():
        total = jnp.zeros((ROWS, TOK), F32)
        for j in range(G):
            total += jnp.dot(
                wv[:, j * 768 : (j + 1) * 768], xt[j].reshape(768, TOK), preferred_element_type=F32
            )
        proj[...] = total.astype(BF16)
        x2[r] = xt[r]

    def swap_grads():
        arrived(oga.at[0:7], og_r)
        send(oga, ogx, ox_s, ox_r, core_dev)

    def products(mine):
        arrived(ogx, ox_r)
        rows = jnp.concatenate(
            [jnp.concatenate([grads[k] for k in range(R)], axis=1) for grads in (ogx, oga)], axis=0
        )
        for i, d in enumerate(mine):
            p = near[d]
            for k in range(1, R):
                rr = (r + k) % R
                arrived(x2.at[rr, p], x_r.at[rr, i])
            columns = jnp.concatenate([x2[k, p].reshape(S * FB, TOK) for k in range(R)], axis=1)
            both = dot_nt(rows, columns)
            wgx[i] = both[:ROWS]
            send(wgx.at[i], wgp.at[p], wx_s, wx_r, core_dev)
            wgp[p] = both[ROWS:]

    def collect():
        arrived(wgp.at[0:2], wx_r)
        for p in range(Q):
            wg[:, p * S * FB : (p + 1) * S * FB] = wgp[p]

    @pl.when(c == 0)
    def _():
        xt[g, q, yl, 0] = own_ctx[...]

    def answer():
        for gp in range(G):

            @pl.when(below(gp) & beside(gp))
            def _():
                greet(ok.at[g], at(gp, q))

    def admitted(step):
        for gp in range(G):

            @pl.when(above(gp) & ((gp - g + 8) % 8 == step % 8))
            def _():
                pl.semaphore_wait(ok.at[gp], 1)

    @pl.when(c == 0)
    def _():
        answer()
        for i, d in enumerate(order):
            send(pc.at[near[d]], rc.at[near[d]], rc_s, rc_r.at[i], core_dev)
        arrived(xt.at[g, q, yl, 1], cx_r)
        for gp in range(3):
            jump(gp, start)

        def first_hop(step):
            admitted(step)
            hop(0, step, start)

        @pl.when(g == 0)
        def _():
            first_hop(1)

        first_hop(-1)

        @pl.when(g > 0)
        def _():
            first_hop(1)

        share_grads()

        @pl.when(g < 4)
        def _():
            rounds(lambda b: b < 4)
            far_done(0)
            rounds(lambda b: b >= 4)
            far_done(1)

        @pl.when(g >= 4)
        def _():
            rounds(lambda b: b != (g + 4) % 8)
            far_done(1)
            rounds(lambda b: b == (g + 4) % 8)
            far_done(0)

        pair_arrived(0, 0)
        near_arrived(0)
        pair_arrived(0, 1)
        near_arrived(1)
        pair_done(0)
        pair_done(1)
        swap_grads()
        for k in range(4):
            hop(k, 1, wait_sent)
            hop(k, -1, wait_sent)
        for gp in range(3):
            jump(gp, wait_sent)
        for h in range(2):
            near_sends(h, wait_sent)
        sent(pc, rc_s)
        sent(oga.at[0:7], og_s)
        project()
        sent(x2.at[0:4], a_s)
        sent(x2, b_s)
        sent(oga, ox_s)
        products(held[0])
        arrived(cg_half, cg_r)
        cg[...] = cg_half[...]
        collect()
        sent(x2.at[0:7], x_s)
        sent(wgx, wx_s)

    legs = ((1, 1), (1, -1), (2, 1), (2, -1), (3, 1), (3, -1), (4, 1))

    def leg(k, step):
        last = 4 if step == 1 else 3
        target = (g + step * (last + 1 - k) + 8) % 8
        whole = (target > 3) | ((target == 3) & (step == -1))
        goes = whole | (g < 4)
        fed = whole | ((g - step >= 0) & (g - step < 4))
        return (k - 1 if step == 1 else 3 + k), target, goes, fed

    def rs_copy(slot, there, device):
        return copy_of(fsend.at[slot], frecv.at[there], rf_s.at[slot], rf_r.at[there], device)

    def owner_sum():
        for slot, here in [(6, g >= 0), (3, g != 0)] + [(b + 3, g < 3) for b in range(4, 8)]:

            @pl.when(here)
            def _():
                arrived(frecv.at[slot], rf_r.at[slot])
                pf[q, g, yl] += frecv[slot].astype(F32)

        total = pf[q, g, yl].astype(BF16)
        sent(own_ctx, one_s.at[0])
        cg_half[...] = total[0]
        send(cg_half, cg_half, one_s.at[1], cg_r, core_dev)
        cg[...] = total[1]

    @pl.when(c == 1)
    def _():
        send(own_ctx, xt.at[g, q, yl, 1], one_s.at[0], cx_r, core_dev)
        answer()
        share_grads()
        for i, d in enumerate(order):
            cls = near[d]
            arrived(rc.at[cls], rc_r.at[i])
            ysend[cls] = (pf[cls, :, 1 - yl] + rc[cls, :, 1 - yl].astype(F32)).astype(BF16)
            send(ysend.at[cls], yrecv.at[cls], ry_s, ry_r.at[i], y_dev)
        for i, d in enumerate(order):
            cls = near[d]
            arrived(yrecv.at[cls], ry_r.at[i])
            total = pf[cls, :, yl] + rc[cls, :, yl].astype(F32) + yrecv[cls].astype(F32)
            if d == 0:
                pf[cls, :, yl] = total
            else:
                nsend[d - 1] = total.astype(BF16)
                if d == 2:
                    i0, i1 = jnp.where(z < 2, 4, 2), jnp.where(z > 29, 4, 2)
                    send(nsend.at[1, 0:4], nrecv.at[i0, 0:4], rn_s, rn_r.at[i0], at_z(jnp.where(z < 2, z + 2, z - 2)))
                    i2 = jnp.where(z > 29, 4, 5)
                    send(nsend.at[1, 4:8], nrecv.at[i1, 4:8], rn_s, rn_r.at[i2], at_z(jnp.where(z > 29, z - 2, z + 2)))
                elif d == 1:
                    i0 = jnp.where(z == 31, 3, 1)
                    send(nsend.at[0], nrecv.at[i0], rn_s, rn_r.at[i0], at_z(jnp.where(z == 31, z - 3, z + 1)))
                else:
                    i0 = jnp.where(z == 0, 3, 0)
                    send(nsend.at[2], nrecv.at[i0], rn_s, rn_r.at[i0], at_z(jnp.where(z == 0, z + 3, z - 1)))
        for here, ref, sem in (
            (z < 31, nrecv.at[0], 0),
            (z > 0, nrecv.at[1], 1),
            (z < 30, nrecv.at[2, 0:4], 2),
            (z > 1, nrecv.at[2, 4:8], 5),
        ):

            @pl.when(here)
            def _():
                arrived(ref, rn_r.at[sem])

            @pl.when(jnp.logical_not(here))
            def _():
                ref[...] = jnp.zeros(ref.shape, BF16)

        window = pf[q, :, yl] + nrecv[0].astype(F32) + nrecv[1].astype(F32) + nrecv[2].astype(F32)
        pf[q, :, yl] = window
        for here, ref, sem, low, high in (
            ((z == 3) | (z == 28), nrecv.at[3], 3, 0, 8),
            ((z == 2) | (z == 3), nrecv.at[4, 0:4], 4, 0, 4),
            ((z == 28) | (z == 29), nrecv.at[4, 4:8], 4, 4, 8),
        ):

            @pl.when(here)
            def _():
                arrived(ref, rn_r.at[sem])
                pf[q, low:high, yl] += ref[...].astype(F32)

        admitted(1)
        admitted(-1)
        for gp in range(3):

            @pl.when(g >= 4)
            def _():
                fsend[7 + gp] = pf[q, gp, yl].astype(BF16)
                rs_copy(7 + gp, 3 + g, at(gp, q)).start()

        def pass_on(k, step, early):
            slot, target, goes, fed = leg(k, step)
            goes = goes & early(target)

            @pl.when(goes)
            def _():
                fsend[slot] = pf[q, target, yl].astype(BF16)

            if (k, step) == (1, -1):

                @pl.when(goes & (g == 6))
                def _():
                    arrived(frecv.at[11], rf_r.at[11])
                    fsend[slot] = (pf[q, target, yl] + frecv[11].astype(F32)).astype(BF16)

            if k > 1:

                @pl.when(goes & fed)
                def _():
                    arrived(frecv.at[slot - 1], rf_r.at[slot - 1])
                    fsend[slot] = (pf[q, target, yl] + frecv[slot - 1].astype(F32)).astype(BF16)

            @pl.when(goes)
            def _():
                rs_copy(slot, slot, at((g + step + 8) % 8, q)).start()

        for k, step in legs[:2]:
            pass_on(k, step, lambda target: target != 3)

        @pl.when(g == 7)
        def _():
            fsend[10] = pf[q, 3, yl].astype(BF16)
            rs_copy(10, 11, at(6, q)).start()

        for k, step in legs[2:]:
            pass_on(k, step, lambda target: target != 3)
        for k, step in legs:
            pass_on(k, step, lambda target: target == 3)

        swap_grads()
        sent(ysend, ry_s)
        sent(nsend, rn_s)
        sent(oga.at[0:7], og_s)
        for h in range(2):
            arrived(xt.at[half(h), :, yl], ca_r.at[h])
            arrived(xt.at[half(h), :, 1 - yl], cb_r.at[h])
        project()
        for gp in range(3):

            @pl.when(g >= 4)
            def _():
                rs_copy(7 + gp, 3 + g, at(gp, q)).wait_send()

        for k, step in legs:
            slot, target, goes, fed = leg(k, step)

            @pl.when(goes)
            def _():
                rs_copy(slot, slot, at((g + step + 8) % 8, q)).wait_send()

        @pl.when(g == 7)
        def _():
            rs_copy(10, 11, at(6, q)).wait_send()

        @pl.when(g >= 4)
        def _():
            owner_sum()

        products(held[1])

        @pl.when(g < 4)
        def _():
            owner_sum()

        collect()
        sent(cg_half, one_s.at[1])
        sent(oga, ox_s)
        sent(wgx, wx_s)


def local(context, w_out, out_grad):
    vmem = pl.BlockSpec(memory_space=pltpu.VMEM)
    dma = pltpu.SemaphoreType.DMA
    projected, context_grad, weight_grad = pl.pallas_call(
        kernel,
        out_shape=(
            jax.ShapeDtypeStruct((ROWS, TOK), BF16),
            jax.ShapeDtypeStruct((FB, TOK), BF16),
            jax.ShapeDtypeStruct((ROWS, Q * S * FB), F32),
        ),
        in_specs=[pl.BlockSpec(memory_space=pltpu.HBM)] * 2,
        out_specs=(vmem,) * 3,
        scratch_shapes=[
            pltpu.VMEM((G, Q, 2, 2, FB, TOK), BF16),
            pltpu.VMEM((ROWS, G * Q * S * FB), BF16),
            pltpu.VMEM((Q, G, 2, 2, FB, TOK), F32),
            pltpu.VMEM((Q, G, 2, 2, FB, TOK), BF16),
            pltpu.VMEM((Q, G, 2, 2, FB, TOK), BF16),
            pltpu.VMEM((Q, G, 2, FB, TOK), BF16),
            pltpu.VMEM((Q, G, 2, FB, TOK), BF16),
            pltpu.VMEM((3, G, 2, FB, TOK), BF16),
            pltpu.VMEM((5, G, 2, FB, TOK), BF16),
            pltpu.VMEM((11, 2, FB, TOK), BF16),
            pltpu.VMEM((12, 2, FB, TOK), BF16),
            pltpu.VMEM((R, ROWS, TOK), BF16),
            pltpu.VMEM((R, Q, 2, 2, FB, TOK), BF16),
            pltpu.VMEM((FB, TOK), BF16),
            pltpu.VMEM((FB, TOK), BF16),
            pltpu.VMEM((R, ROWS, TOK), BF16),
            pltpu.VMEM((Q, ROWS, S * FB), F32),
            pltpu.VMEM((2, ROWS, S * FB), F32),
            pltpu.SemaphoreType.REGULAR((G,)), dma((3,)),
            dma, dma((6, 2)), dma, dma, dma, dma, dma, dma, dma, dma((11,)), dma((11,)), dma, dma((2,)),
            dma((G,)), dma((3, 2)), dma((Q, 2)), dma((2,)), dma((2,)), dma, dma((R, 2)), dma, dma, dma((Q,)), dma((Q,)),
            dma((6,)), dma((12,)), dma, dma,
        ],
        compiler_params=pltpu.CompilerParams(
            collective_id=0, has_side_effects=True, vmem_limit_bytes=52 * 2**20
        ),
        cost_estimate=pl.CostEstimate(
            flops=6 * TOK * ROWS * 6144, bytes_accessed=4_000_000, transcendentals=0
        ),
    )(jnp.concatenate([out_grad.T, context.T], axis=0), w_out)
    return projected.T, context_grad.T, weight_grad


def solution(mesh):
    placed = (P("dp", "tensor"), P("tensor", None), P("dp", "tensor"))
    return jax.shard_map(
        local,
        mesh=mesh,
        in_specs=placed,
        out_specs=(P("dp", "tensor"), P("dp", "tensor"), P("tensor", "dp")),
        check_vma=False,
    )
```
